256 devices in a mesh: row: 8 (over z_hi, y), col: 32 (over x, z_lo, core).
Axes of the slice: x: 4, y: 4, z: 8 (z_hi: 2, z_lo: 4; z = z_hi * 4 + z_lo), core: 2. Of those that a mesh axis runs over, the one named last changes fastest.
Arguments:
- patches: bfloat16 [32768, 768], P(('row', 'col')), may hold values from -4 to 4
- tile_slot: int32 [32768], P(('row', 'col')), may hold values from 0 to 127, as said below
- w_embed: bfloat16 [768, 1024], replicated, may hold values from -0.21875 to 0.21875
- w_query: bfloat16 [1024, 1024], replicated, may hold values from -0.1875 to 0.1875
- w_keyval: bfloat16 [1024, 2048], replicated, may hold values from -0.1875 to 0.1875
- w_out: bfloat16 [1024, 1024], replicated, may hold values from -0.1875 to 0.1875
- cotangent: bfloat16 [128, 256, 1024], P('row', 'col'), may hold values from -6 to 6
Outputs:
- final_tokens: bfloat16 [128, 256, 1024], P('row', 'col')
- input_grad: bfloat16 [128, 256, 1024], P('row', 'col')
The draws below stay inside these ranges and needn't reach their ends.
Inputs may be any that keep to these rules, and one draw needn't show every extreme that they name: `tile_slot`: row i of the 128 embedding rows held by the device at (row r, col c) goes to the core tile in grid tile row i // 16 and tile column c; for every core tile the slots named by its 8 sources are together each position 0 to 127 exactly once.
All inputs are finite; a program needn't handle non-finite values.
Results may differ from the reference program's by a relative error of at most 0.014.
Values may be sent and summed in bfloat16 or wider, within the bound.
No kernel may reach another device: no remote copies, remote signals or barrier semaphores. Data moves between devices by JAX's collectives and lax.ppermute only.
A program may use at most 192 MiB of HBM per device.

```python
import jax
import jax.numpy as jnp
from jax import lax

D = 1024
HEADS = 16
PIX = 768
LOOPS = 2
TR = 16
TC = 8
TILE = 128
PER = 16
GR = 128
GC = 256
TOKENS = 32768
N_ROW = 8
N_COL = 32


def draw_patches(key, part):
    key = jax.random.fold_in(key, 11)
    base_key = jax.random.fold_in(key, 0)
    values = jnp.clip(jax.random.normal(base_key, (TOKENS, PIX), jnp.float32), -4.0, 4.0)
    return values.astype(jnp.bfloat16)


def draw_tile_slot(key, part):
    key = jax.random.fold_in(key, 23)
    tile_keys = jax.random.split(key, N_ROW * N_COL)
    shuffles = jax.vmap(lambda one_key: jax.random.permutation(one_key, TILE))(tile_keys)
    arranged = shuffles.reshape(N_ROW, N_COL, N_ROW, PER).transpose(2, 1, 0, 3)
    return arranged.reshape(TOKENS).astype(jnp.int32)


def shard_levels(own_key, shape, pieces, least, top_value):
    def one(dim, shards_of):
        draws = jax.random.uniform(jax.random.fold_in(jax.random.fold_in(own_key, 6), dim), (shards_of,), jnp.float32, least / len(pieces), top_value / len(pieces))
        return jnp.repeat(jnp.exp(draws), shape[dim] // shards_of).reshape((-1,) + (1,) * (len(shape) - dim - 1))

    level = one(*pieces[0])
    for cut in pieces[1:]:
        level = level * one(*cut)
    return level


def gaussian(key, shape, spread, limit, shards=(), kind=jnp.bfloat16):
    gain = shard_levels(key, shape, shards, -0.22, 0.18) if shards else 1.0
    entries = jax.random.normal(key, shape, jnp.float32) * spread * gain
    return jnp.minimum(jnp.maximum(entries, -limit), limit).astype(kind)


def setup_inputs(seed: int = 0) -> dict:
    arg_keys = jax.random.split(jax.random.key(seed), 8)
    return {
        "patches": draw_patches(jax.random.fold_in(arg_keys[7], 71), 0),
        "tile_slot": draw_tile_slot(jax.random.fold_in(arg_keys[7], 71), 0),
        "w_embed": gaussian(arg_keys[2], (PIX, D), PIX ** -0.5, 0.21875),
        "w_query": gaussian(arg_keys[3], (D, D), D ** -0.5, 0.1875),
        "w_keyval": gaussian(arg_keys[4], (D, 2 * D), D ** -0.5, 0.1875),
        "w_out": gaussian(arg_keys[5], (D, D), D ** -0.5, 0.1875),
        "cotangent": gaussian(arg_keys[6], (GR, GC, D), 1.0, 6.0, ((0, 8), (1, 32))),
    }


EPSILON = 1e-06

def rms_scale(values):
    return values * lax.rsqrt(lax.optimization_barrier(jnp.mean(values * values, axis=-1, keepdims=True)) + EPSILON)

def head_scale(values):
    shaped = values.reshape(values.shape[:-1] + (HEADS, D // HEADS))
    return rms_scale(shaped).reshape(values.shape)

def project_query(normed, w_query):
    flattened = normed.reshape(-1, D)
    projected = jnp.dot(flattened, w_query, preferred_element_type=jnp.float32)
    return head_scale(projected).astype(jnp.bfloat16).reshape(normed.shape)

def project_keyval(normed, w_keyval):
    flattened = normed.reshape(-1, D)
    projected = jnp.dot(flattened, w_keyval, preferred_element_type=jnp.float32)
    key_part = head_scale(projected[:, :D]).astype(jnp.bfloat16)
    value_part = projected[:, D:].astype(jnp.bfloat16)
    joined = jnp.concatenate([key_part, value_part], axis=1)
    return joined.reshape(normed.shape[:-1] + (2 * D,))

def neighbourhood(queries, keyval_wide):
    head_size = D // HEADS
    score_scale = head_size ** (-0.5)
    padded = jnp.pad(keyval_wide, ((3, 3), (3, 3), (0, 0)))
    row_number = jnp.arange(GR + 6, dtype=jnp.int32)
    row_valid = ((row_number >= 3) & (row_number < GR + 3)).astype(jnp.float32)
    col_number = jnp.arange(GC + 6, dtype=jnp.int32)
    col_valid = ((col_number >= 3) & (col_number < GC + 3)).astype(jnp.float32)

    def one_row(row_index):
        query_row = lax.dynamic_index_in_dim(queries, row_index, 0, keepdims=False)
        query_row = query_row.astype(jnp.float32).reshape(GC, HEADS, head_size)
        window_rows = lax.dynamic_slice_in_dim(padded, row_index, 7, 0)
        valid_rows = lax.dynamic_slice_in_dim(row_valid, row_index, 7, 0)
        weights = []
        denominator = jnp.zeros((GC, HEADS), jnp.float32)
        for row_off in range(7):
            for col_off in range(7):
                key_view = window_rows[row_off, col_off:col_off + GC, :D].reshape(GC, HEADS, head_size)
                scores = lax.optimization_barrier(jnp.sum(query_row * key_view, axis=-1)) * score_scale
                window_mask = valid_rows[row_off] * col_valid[col_off:col_off + GC]
                weight = jnp.exp(scores) * window_mask[:, None]
                weights.append(weight)
                denominator = denominator + weight
        accumulated = jnp.zeros((GC, HEADS, head_size), jnp.float32)
        position = 0
        for row_off in range(7):
            for col_off in range(7):
                value_view = window_rows[row_off, col_off:col_off + GC, D:].reshape(GC, HEADS, head_size)
                accumulated = accumulated + (weights[position] / denominator)[:, :, None] * value_view
                position = position + 1
        return accumulated.reshape(GC, D)
    return lax.map(jax.checkpoint(one_row), jnp.arange(GR, dtype=jnp.int32))

def core_step(tokens_in, w_query, w_keyval, w_out):
    residual = tokens_in.astype(jnp.float32)
    normed = rms_scale(residual).astype(jnp.bfloat16)
    queries = project_query(normed, w_query)
    keyval = project_keyval(normed, w_keyval).astype(jnp.float32)
    attended = neighbourhood(queries, keyval).astype(jnp.bfloat16)
    update = jnp.dot(attended.reshape(-1, D), w_out, preferred_element_type=jnp.float32).reshape(residual.shape)
    return (residual + update).astype(jnp.bfloat16)

def reference(patches, tile_slot, w_embed, w_query, w_keyval, w_out, cotangent):
    embedded = jnp.dot(patches, w_embed, preferred_element_type=jnp.float32).astype(jnp.bfloat16)
    row_number = jnp.arange(TOKENS, dtype=jnp.int32)
    column_block = row_number // TILE % N_COL
    dest_row = row_number % TILE // PER
    target = ((dest_row * N_COL + column_block) * TILE + tile_slot).astype(jnp.int32)
    placed = jnp.zeros((TOKENS, D), jnp.bfloat16).at[target].set(embedded)
    token_grid = placed.reshape(N_ROW, N_COL, TR, TC, D).transpose(0, 2, 1, 3, 4).reshape(GR, GC, D)

    def looped(tokens_in):
        return core_step(tokens_in, w_query, w_keyval, w_out)
    current = token_grid
    for loop_index in range(LOOPS - 1):
        current = looped(current)
    final_tokens, pull_back = jax.vjp(looped, current)
    input_grad, = pull_back(cotangent)
    return (final_tokens, input_grad)
```

```python
import functools

import jax
import jax.numpy as jnp
from jax import lax
from jax.experimental import pallas as pl
from jax.experimental.pallas import tpu as pltpu
from jax.sharding import PartitionSpec as P

D = 1024
PIX = 768
EPSILON = 1e-06
F32 = jnp.float32
BF = jnp.bfloat16
LANES = 256
GROUPS = D // LANES
NT = (((1,), (1,)), ((), ()))
NN = (((1,), (0,)), ((), ()))
TN = (((0,), (0,)), ((), ()))


def dot(a, b, dims=NN):
    return lax.dot_general(a, b, dims, preferred_element_type=F32)


def iota(shape, axis):
    return lax.broadcasted_iota(jnp.int32, shape, axis)


def group_mean_matrix():
    same = (iota((LANES, LANES), 0) >> 6) == (iota((LANES, LANES), 1) >> 6)
    return jnp.where(same, 1.0 / 64, 0.0).astype(BF)


def group_mean(values, means):
    return dot(values.astype(BF), means)


def row_scale(residual):
    return lax.rsqrt(jnp.mean(residual * residual, axis=-1, keepdims=True) + EPSILON)


def cols(index):
    return pl.ds(pl.multiple_of(index * LANES, LANES), LANES)


def head_masks():
    lane = iota((1, LANES), 1) >> 6
    return [jnp.where(lane == h, 1.0, 0.0).astype(BF) for h in range(4)]


def stack_heads(values, masks):
    return jnp.concatenate([values * mask for mask in masks], axis=0)


def unstack_heads(stacked):
    lane = iota((64, LANES), 1) >> 6
    parts = [stacked[64 * h : 64 * h + 64] for h in range(4)]
    low = jnp.where(lane == 0, parts[0], parts[1])
    high = jnp.where(lane == 2, parts[2], parts[3])
    return jnp.where(lane < 2, low, high)


def block_mask(first_row, col_index, grid_rows, grid_cols):
    shape = (64, 256)
    token, key = iota(shape, 0), iota(shape, 1)
    query_row, query_col = token >> 3, token & 7
    side = key - 128
    left = key < 192
    rim = side & 63
    key_row = jnp.where(key < 128, key >> 3, rim >> 2)
    rim_col = jnp.where(left, (rim & 3) - 4, (rim & 3) + 8)
    key_col = jnp.where(key < 128, key & 7, rim_col)
    row_gap = key_row - query_row - 4
    col_gap = key_col - query_col
    near = (row_gap >= -3) & (row_gap <= 3) & (col_gap >= -3) & (col_gap <= 3)
    row = first_row + key_row
    col = col_index * 8 + key_col
    inside = (row >= 0) & (row < grid_rows) & (col >= 0) & (col < grid_cols)
    mask = jnp.where(near & inside, 1.0, 0.0)
    return jnp.concatenate([mask] * 4, axis=0)


def softmax_parts(scores, mask):
    weight = jnp.exp(scores) * mask
    total = jnp.sum(weight, axis=-1, keepdims=True)
    return weight, 1.0 / jnp.where(total > 0, total, 1.0)


def place_kernel(recv_ref, own_ref, left_ref, right_ref):
    sources, slots = [], []
    for tile in range(3):
        part = recv_ref[:, 16 * tile : 16 * tile + 16, :].reshape(128, PIX + 128)
        sources.append(part[:, :PIX])
        slot = part[:, PIX:].astype(F32).T + 128.0 * tile
        slots.append(slot[:8])
    source = jnp.concatenate(sources, axis=0)
    slot = jnp.concatenate(slots, axis=1)

    def pick(position):
        hot = jnp.where(position == slot[:1], 1.0, 0.0).astype(BF)
        return dot(hot, source).astype(BF)

    own_ref[...] = pick((iota((320, 384), 0) + 32).astype(F32))
    n = iota((144, 384), 0)
    edge = ((n >> 2) + 6) * 8 + (n & 3)
    left_ref[...] = pick(edge.astype(F32))
    right_ref[...] = pick((edge + 4).astype(F32))


def own_first_kernel(own_ref, we_ref, wq_ref, wkv_ref, x0_ref, q_ref, kv_ref, x_s, n_s):
    means = group_mean_matrix()

    @pl.loop(0, GROUPS)
    def _(g):
        x_s[:, cols(g)] = dot(own_ref[...], we_ref[:, cols(g)]).astype(BF).astype(F32)

    residual = x_s[...]
    n_s[...] = (residual * row_scale(residual)).astype(BF)
    x0_ref[...] = residual[32:288].astype(BF)

    @pl.loop(0, GROUPS)
    def _(g):
        query = dot(n_s[32:288, :], wq_ref[:, cols(g)])
        query = query * lax.rsqrt(group_mean(query * query, means) + EPSILON)
        q_ref[:, cols(g)] = (query.astype(BF) * 0.125).astype(BF)
        key = dot(n_s[...], wkv_ref[:, cols(g)])
        key = key * lax.rsqrt(group_mean(key * key, means) + EPSILON)
        kv_ref[:, cols(g)] = key.astype(BF)
        kv_ref[:, cols(g + GROUPS)] = dot(n_s[...], wkv_ref[:, cols(g + GROUPS)]).astype(BF)


def keys_of(kv_ref, rim_ref, block, group):
    rim = rim_ref.shape[0] // 2
    lanes = cols(group)
    return jnp.concatenate(
        [
            kv_ref[64 * block : 64 * block + 128, lanes],
            rim_ref[32 * block : 32 * block + 64, lanes],
            rim_ref[rim + 32 * block : rim + 32 * block + 64, lanes],
        ],
        axis=0,
    )


def padded_rim(values):
    half = values.shape[0] // 2
    pad = jnp.zeros((8, values.shape[1]), F32)
    return jnp.concatenate([pad, values[:half], pad, pad, values[half:], pad], axis=0)


def first_core_kernel(
    grid_rows, grid_cols,
    place_ref, left_ref, right_ref, we_ref, wkv_ref, wo_ref, x0_ref, q_ref, kv_ref,
    x1_ref, go_left_ref, go_right_ref,
    p_s, x_s, n_s, rim_s, o_s, mask_s,
):
    means = group_mean_matrix()
    p_s[0:144, :] = left_ref[...]
    p_s[144:288, :] = right_ref[...]

    @pl.loop(0, GROUPS)
    def _(g):
        x_s[:, cols(g)] = dot(p_s[...], we_ref[:, cols(g)]).astype(BF).astype(F32)

    residual = x_s[...]
    n_s[...] = (residual * row_scale(residual)).astype(BF)

    @pl.loop(0, GROUPS)
    def _(g):
        key = dot(n_s[...], wkv_ref[:, cols(g)])
        key = key * lax.rsqrt(group_mean(key * key, means) + EPSILON)
        rim_s[:, cols(g)] = padded_rim(key).astype(BF)
        value = dot(n_s[...], wkv_ref[:, cols(g + GROUPS)])
        rim_s[:, cols(g + GROUPS)] = padded_rim(value).astype(BF)

    first_row = place_ref[0] * 16 - 12
    for block in range(4):
        mask_s[block] = block_mask(first_row + 8 * block, place_ref[1], grid_rows, grid_cols)
    masks = head_masks()

    @pl.loop(0, GROUPS)
    def _(g):
        for block in range(4):
            query = stack_heads(q_ref[64 * block : 64 * block + 64, cols(g)], masks)
            key = keys_of(kv_ref, rim_s, block, g)
            value = keys_of(kv_ref, rim_s, block, g + GROUPS)
            weight, inverse = softmax_parts(dot(query, key, NT), mask_s[block])
            mixed = dot(weight.astype(BF), value) * inverse
            o_s[64 * block : 64 * block + 64, cols(g)] = unstack_heads(mixed).astype(BF)

    n = iota((112, 256), 0)
    edge = ((n >> 2) + 2) * 8 + (n & 3)
    source = iota((112, 256), 1)
    pick_left = jnp.where(edge == source, 1.0, 0.0).astype(BF)
    pick_right = jnp.where(edge + 4 == source, 1.0, 0.0).astype(BF)

    @pl.loop(0, GROUPS)
    def _(g):
        total = x0_ref[:, cols(g)].astype(F32) + dot(o_s[...], wo_ref[:, cols(g)])
        total = total.astype(BF)
        x1_ref[:, cols(g)] = total
        go_left_ref[:, cols(g)] = dot(pick_left, total).astype(BF)
        go_right_ref[:, cols(g)] = dot(pick_right, total).astype(BF)


def own_second_kernel(
    x1_ref, cot_ref, above_ref, below_ref, wq_ref, wkv_ref, wo_ref,
    q_ref, kv_ref, do_ref, rsq_ref, rsk_ref,
    n_s, c_s,
):
    means = group_mean_matrix()
    residual = x1_ref[...].astype(F32)
    n_s[...] = (residual * row_scale(residual)).astype(BF)
    c_s[0:32, :] = above_ref[...]
    c_s[32:160, :] = cot_ref[...]
    c_s[160:192, :] = below_ref[...]

    @pl.loop(0, GROUPS)
    def _(g):
        query = dot(n_s[32:224, :], wq_ref[:, cols(g)])
        scale = lax.rsqrt(group_mean(query * query, means) + EPSILON)
        q_ref[:, cols(g)] = ((query * scale).astype(BF) * 0.125).astype(BF)
        rsq_ref[:, cols(g)] = scale[32:160]
        key = dot(n_s[...], wkv_ref[:, cols(g)])
        scale = lax.rsqrt(group_mean(key * key, means) + EPSILON)
        kv_ref[:, cols(g)] = (key * scale).astype(BF)
        rsk_ref[:, cols(g)] = scale[64:192]
        kv_ref[:, cols(g + GROUPS)] = dot(n_s[...], wkv_ref[:, cols(g + GROUPS)]).astype(BF)
        do_ref[:, cols(g)] = dot(c_s[...], wo_ref[cols(g), :], NT).astype(BF)


def head_scale_back(back, normed, scale, means):
    return scale * (back - normed * group_mean(back * normed, means))


def second_core_kernel(
    grid_rows, grid_cols,
    place_ref, left_ref, right_ref, wkv_ref, q_ref, kv_ref, do_ref,
    o_ref, dq_ref, dkv_ref, go_left_ref, go_right_ref,
    n_s, rim_s, rs_s, db_s, mask_s,
):
    means = group_mean_matrix()
    residual = jnp.concatenate([left_ref[...].astype(F32), right_ref[...].astype(F32)], axis=0)
    residual = padded_rim(residual)
    n_s[...] = (residual * row_scale(residual)).astype(BF)

    @pl.loop(0, GROUPS)
    def _(g):
        key = dot(n_s[...], wkv_ref[:, cols(g)])
        scale = lax.rsqrt(group_mean(key * key, means) + EPSILON)
        rim_s[:, cols(g)] = (key * scale).astype(BF)
        rs_s[0:64, cols(g)] = scale[32:96]
        rs_s[64:128, cols(g)] = scale[160:224]
        rim_s[:, cols(g + GROUPS)] = dot(n_s[...], wkv_ref[:, cols(g + GROUPS)]).astype(BF)

    first_row = place_ref[0] * 16 - 8
    for block in range(3):
        mask_s[block] = block_mask(first_row + 8 * block, place_ref[1], grid_rows, grid_cols)
    masks = head_masks()

    @pl.loop(0, GROUPS)
    def _(g):
        key_backs, value_backs = [], []
        for block in range(3):
            query = stack_heads(q_ref[64 * block : 64 * block + 64, cols(g)], masks)
            key = keys_of(kv_ref, rim_s, block, g)
            value = keys_of(kv_ref, rim_s, block, g + GROUPS)
            weight, inverse = softmax_parts(dot(query, key, NT), mask_s[block])
            probs = weight * inverse
            probs_low = probs.astype(BF)
            out_back = stack_heads(do_ref[64 * block : 64 * block + 64, cols(g)], masks)
            probs_back = dot(out_back, value, NT)
            centre = jnp.sum(probs_back * probs, axis=-1, keepdims=True)
            scores_back = (probs * (probs_back - centre)).astype(BF)
            o_ref[64 * block : 64 * block + 64, cols(g)] = unstack_heads(
                dot(probs_low, value)
            ).astype(BF)
            dq_ref[64 * block : 64 * block + 64, cols(g)] = unstack_heads(
                dot(scores_back, key)
            ).astype(BF)
            key_backs.append(dot(scores_back, query, TN))
            value_backs.append(dot(probs_low, out_back, TN))

        def fold(parts):
            def piece(start, half):
                return jnp.concatenate(
                    [
                        parts[0][start + half : start + 2 * half] + parts[1][start : start + half],
                        parts[1][start + half : start + 2 * half] + parts[2][start : start + half],
                    ],
                    axis=0,
                )

            return piece(0, 64), jnp.concatenate([piece(128, 32), piece(192, 32)], axis=0)

        own, rim = fold(key_backs)
        dkv_ref[:, cols(g)] = own.astype(BF)
        normed = jnp.concatenate([rim_s[32:96, cols(g)], rim_s[160:224, cols(g)]], axis=0)
        rim = head_scale_back(rim, normed.astype(F32), rs_s[:, cols(g)], means)
        db_s[:, cols(g)] = rim.astype(BF)
        own, rim = fold(value_backs)
        dkv_ref[:, cols(g + GROUPS)] = own.astype(BF)
        db_s[:, cols(g + GROUPS)] = rim.astype(BF)

    @pl.loop(0, GROUPS)
    def _(g):
        back = dot(db_s[...], wkv_ref[cols(g), :], NT).astype(BF)
        go_left_ref[:, cols(g)] = back[:64]
        go_right_ref[:, cols(g)] = back[64:]


def own_back_kernel(
    x1_ref, o_ref, dq_ref, dkv_ref, q_ref, kv_ref, rsq_ref, rsk_ref, wq_ref, wkv_ref, wo_ref,
    out_ref, dn_ref,
    a_s, b_s,
):
    means = group_mean_matrix()

    @pl.loop(0, GROUPS)
    def _(g):
        total = x1_ref[64:192, cols(g)].astype(F32) + dot(o_ref[32:160, :], wo_ref[:, cols(g)])
        out_ref[:, cols(g)] = total.astype(BF)
        back = dq_ref[32:160, cols(g)].astype(F32) * 0.125
        normed = q_ref[32:160, cols(g)].astype(F32) * 8.0
        a_s[:, cols(g)] = head_scale_back(back, normed, rsq_ref[:, cols(g)], means).astype(BF)
        back = dkv_ref[:, cols(g)].astype(F32)
        normed = kv_ref[64:192, cols(g)].astype(F32)
        b_s[:, cols(g)] = head_scale_back(back, normed, rsk_ref[:, cols(g)], means).astype(BF)
        b_s[:, cols(g + GROUPS)] = dkv_ref[:, cols(g + GROUPS)]

    @pl.loop(0, GROUPS)
    def _(g):
        back = dot(a_s[...], wq_ref[cols(g), :], NT) + dot(b_s[...], wkv_ref[cols(g), :], NT)
        dn_ref[:, cols(g)] = back


def last_kernel(x1_ref, cot_ref, dn_ref, left_ref, right_ref, out_ref):
    n, source = iota((128, 64), 0), iota((128, 64), 1)
    column = n & 7
    place = (n >> 3) * 4 + (column & 3)
    from_left = jnp.where((place == source) & (column < 4), 1.0, 0.0).astype(BF)
    from_right = jnp.where((place == source) & (column >= 4), 1.0, 0.0).astype(BF)
    pick = jnp.concatenate([from_left, from_right], axis=1)
    arrived = jnp.concatenate([left_ref[...], right_ref[...]], axis=0)
    back = dn_ref[...] + dot(pick, arrived)
    residual = x1_ref[64:192, :].astype(F32)
    scale = row_scale(residual)
    normed = residual * scale
    mean = jnp.mean(back * normed, axis=-1, keepdims=True)
    out_ref[...] = (cot_ref[...].astype(F32) + scale * (back - normed * mean)).astype(BF)


def call(kernel, out_shapes, *operands, scratch=(), flops=0, moved=0, small=None):
    vmem = pl.BlockSpec(memory_space=pltpu.VMEM)
    in_specs = [vmem] * len(operands)
    if small is not None:
        operands = (small,) + operands
        in_specs = [pl.BlockSpec(memory_space=pltpu.SMEM)] + in_specs
    shapes = tuple(jax.ShapeDtypeStruct(s, d) for s, d in out_shapes)
    return pl.pallas_call(
        kernel,
        out_shape=shapes,
        in_specs=in_specs,
        out_specs=tuple(vmem for _ in shapes),
        scratch_shapes=[pltpu.VMEM(s, d) for s, d in scratch],
        compiler_params=pltpu.CompilerParams(vmem_limit_bytes=40 * 1024 * 1024),
        cost_estimate=pl.CostEstimate(flops=flops, bytes_accessed=moved, transcendentals=0),
    )(*operands)


def shift(values, axis, step):
    peers = lax.axis_size(axis)
    return lax.ppermute(
        values, axis, [(i, i + step) for i in range(peers) if 0 <= i + step < peers]
    )


def on_device(patches, tile_slot, w_embed, w_query, w_keyval, w_out, cotangent):
    rows, columns = lax.axis_size("row"), lax.axis_size("col")
    grid_rows, grid_cols = rows * 16, columns * 8
    place = jnp.stack([lax.axis_index("row"), lax.axis_index("col")]).astype(jnp.int32)
    cot = cotangent.reshape(128, D)

    slot = jnp.broadcast_to(tile_slot.astype(BF)[:, None], (128, 128))
    block = jnp.concatenate([patches, slot], axis=1).reshape(rows, 16, PIX + 128)
    wide = jnp.pad(block, ((1, 1), (0, 0), (0, 0)))
    block = jnp.concatenate([wide[:-2], wide[1:-1], wide[2:]], axis=1)
    arrived = lax.all_to_all(block, "row", split_axis=0, concat_axis=0, tiled=True)

    above = shift(cot[96:], "row", 1)
    below = shift(cot[:32], "row", -1)

    own, go_left, go_right = call(
        place_kernel, (((320, PIX), BF), ((144, PIX), BF), ((144, PIX), BF)), arrived
    )
    left = shift(go_right, "col", 1)
    right = shift(go_left, "col", -1)
    x0, queries, keyval = call(
        own_first_kernel,
        (((256, D), BF), ((256, D), BF), ((320, 2 * D), BF)),
        own, w_embed, w_query, w_keyval,
        scratch=(((320, D), F32), ((320, D), BF)),
        flops=8 * 10**9, moved=8 * 10**6,
    )
    x1, go_left, go_right = call(
        functools.partial(first_core_kernel, grid_rows, grid_cols),
        (((256, D), BF), ((112, D), BF), ((112, D), BF)),
        left, right, w_embed, w_keyval, w_out, x0, queries, keyval,
        small=place,
        scratch=(
            ((288, PIX), BF), ((288, D), F32), ((288, D), BF), ((320, 2 * D), BF), ((256, D), BF),
            ((4, 256, 256), F32),
        ),
        flops=8 * 10**9, moved=8 * 10**6,
    )
    left = shift(go_right, "col", 1)
    right = shift(go_left, "col", -1)
    queries, keyval, out_back, query_scale, key_scale = call(
        own_second_kernel,
        (((192, D), BF), ((256, 2 * D), BF), ((192, D), BF), ((128, D), F32), ((128, D), F32)),
        x1, cot, above, below, w_query, w_keyval, w_out,
        scratch=(((256, D), BF), ((192, D), BF)),
        flops=8 * 10**9, moved=8 * 10**6,
    )
    attended, dq, dkv, go_left, go_right = call(
        functools.partial(second_core_kernel, grid_rows, grid_cols),
        (((192, D), BF), ((192, D), BF), ((128, 2 * D), BF), ((64, D), BF), ((64, D), BF)),
        left, right, w_keyval, queries, keyval, out_back,
        small=place,
        scratch=(
            ((256, D), BF), ((256, 2 * D), BF), ((128, D), F32), ((128, 2 * D), BF),
            ((3, 256, 256), F32),
        ),
        flops=8 * 10**9, moved=8 * 10**6,
    )
    left = shift(go_right, "col", 1)
    right = shift(go_left, "col", -1)
    final_tokens, back = call(
        own_back_kernel,
        (((128, D), BF), ((128, D), F32)),
        x1, attended, dq, dkv, queries, keyval, query_scale, key_scale, w_query, w_keyval, w_out,
        scratch=(((128, D), BF), ((128, 2 * D), BF)),
        flops=8 * 10**9, moved=8 * 10**6,
    )
    (input_grad,) = call(last_kernel, (((128, D), BF),), x1, cot, back, left, right)
    return final_tokens.reshape(16, 8, D), input_grad.reshape(16, 8, D)


def solution(mesh):
    in_specs = (
        P(("row", "col"), None),
        P(("row", "col")),
        P(),
        P(),
        P(),
        P(),
        P("row", "col", None),
    )
    out_specs = (P("row", "col", None), P("row", "col", None))
    return jax.shard_map(
        on_device, mesh=mesh, in_specs=in_specs, out_specs=out_specs, check_vma=False
    )
```

```python
import functools

import jax
import jax.numpy as jnp
from jax import lax
from jax.experimental import pallas as pl
from jax.experimental.pallas import tpu as pltpu
from jax.sharding import PartitionSpec as P

D = 1024
PIX = 768
EPSILON = 1e-06
F32 = jnp.float32
BF = jnp.bfloat16
LANES = 256
GROUPS = D // LANES
NT = (((1,), (1,)), ((), ()))
NN = (((1,), (0,)), ((), ()))
TN = (((0,), (0,)), ((), ()))


def dot(a, b, dims=NN):
    return lax.dot_general(a, b, dims, preferred_element_type=F32)


def iota(shape, axis):
    return lax.broadcasted_iota(jnp.int32, shape, axis)


def group_mean_matrix():
    same = (iota((LANES, LANES), 0) >> 6) == (iota((LANES, LANES), 1) >> 6)
    return jnp.where(same, 1.0 / 64, 0.0).astype(BF)


def group_mean(values, means):
    return dot(values.astype(BF), means)


def row_scale(residual):
    return lax.rsqrt(jnp.mean(residual * residual, axis=-1, keepdims=True) + EPSILON)


def cols(index):
    return slice(index * LANES, index * LANES + LANES)


def head_masks():
    lane = iota((1, LANES), 1) >> 6
    return [jnp.where(lane == h, 1.0, 0.0).astype(BF) for h in range(4)]


def stack_heads(values, masks):
    return jnp.concatenate([values * mask for mask in masks], axis=0)


def unstack_heads(stacked):
    lane = iota((64, LANES), 1) >> 6
    parts = [stacked[64 * h : 64 * h + 64] for h in range(4)]
    low = jnp.where(lane == 0, parts[0], parts[1])
    high = jnp.where(lane == 2, parts[2], parts[3])
    return jnp.where(lane < 2, low, high)


def block_mask(first_row, col_index, grid_rows, grid_cols):
    shape = (64, 256)
    token, key = iota(shape, 0), iota(shape, 1)
    query_row, query_col = token >> 3, token & 7
    side = key - 128
    right = (key < 192) == ((col_index & 1) == 0)
    rim = side & 63
    key_row = jnp.where(key < 128, key >> 3, rim >> 2)
    rim_col = jnp.where(right, (rim & 3) + 8, (rim & 3) - 4)
    key_col = jnp.where(key < 128, key & 7, rim_col)
    row_gap = key_row - query_row - 4
    col_gap = key_col - query_col
    near = (row_gap >= -3) & (row_gap <= 3) & (col_gap >= -3) & (col_gap <= 3)
    row = first_row + key_row
    col = col_index * 8 + key_col
    inside = (row >= 0) & (row < grid_rows) & (col >= 0) & (col < grid_cols)
    mask = jnp.where(near & inside, 1.0, 0.0)
    return jnp.concatenate([mask] * 4, axis=0)


def softmax_parts(scores, mask):
    weight = jnp.exp(scores) * mask
    total = jnp.sum(weight, axis=-1, keepdims=True)
    return weight, 1.0 / jnp.where(total > 0, total, 1.0)


def pack_kernel(place_ref, patches_ref, slot_ref, own_ref, far_ref, slot_s, wide_s, sems):
    half = place_ref[0] >> 2
    copies = [pltpu.make_async_copy(slot_ref, slot_s, sems.at[0])]
    for i, (target, side) in enumerate(((own_ref, half), (far_ref, 1 - half))):
        copies.append(
            pltpu.make_async_copy(
                patches_ref.at[pl.ds(pl.multiple_of(48 * side, 16), 80), :],
                target.at[pl.ds(pl.multiple_of(16 - 16 * side, 16), 80), pl.ds(0, PIX)],
                sems.at[i + 1],
            )
        )
    for copy in copies:
        copy.start()
    for copy in copies:
        copy.wait()
    wide_s[...] = jnp.broadcast_to(slot_s[...].astype(F32), (128, 128)).T.astype(BF)
    for target, side in ((own_ref, half), (far_ref, 1 - half)):
        target[pl.ds(pl.multiple_of(80 * side, 16), 16), :] = jnp.zeros((16, PIX + 128), BF)
        target[pl.ds(pl.multiple_of(16 - 16 * side, 16), 80), PIX:] = wide_s[
            pl.ds(pl.multiple_of(48 * side, 16), 80), :
        ]


def windows(place_ref, own_ref, far_ref, step):
    start = pl.multiple_of(((place_ref[0] & 3) ^ step) * 16, 16)
    return own_ref[pl.ds(start, 48), :], far_ref[pl.ds(start, 48), :]


def spread_kernel(place_ref, own_ref, far_ref, touched_ref, *out_refs):
    for step, out_ref in zip((2, 3, 1), out_refs):
        near, far = windows(place_ref, own_ref, far_ref, step)
        out_ref[0:48, :] = near
        out_ref[48:96, :] = far


def place_kernel(
    place_ref, own_in_ref, far_in_ref, in2_ref, in3_ref, in1_ref, own_ref, go_a_ref, go_b_ref
):
    near, far = windows(place_ref, own_in_ref, far_in_ref, 0)
    source = jnp.concatenate([near, far, in2_ref[...], in3_ref[...], in1_ref[...]], axis=0)
    slots = []
    for part in range(3):
        slots.append(source[128 * part : 128 * part + 128, PIX:].astype(F32).T[:8])
    tile = lax.rem(iota((8, 384), 1) >> 4, 3)
    slot = jnp.concatenate(slots, axis=1) + 128.0 * tile.astype(F32)
    source = source[:, :PIX]
    even = 1 - (place_ref[1] & 1)

    def pick(position):
        hot = jnp.where(position.astype(F32) == slot[:1], 1.0, 0.0).astype(BF)
        return dot(hot, source).astype(BF)

    own_ref[...] = pick(iota((320, 384), 0) + 32)
    n = iota((144, 384), 0)
    edge = ((n >> 2) + 6) * 8 + (n & 3)
    go_a_ref[...] = pick(edge + 4 * even)
    go_b_ref[...] = pick(edge + 4 * (1 - even))


def touch_kernel(we_ref, wq_ref, wkv_ref, wo_ref, out_ref):
    total = we_ref[0:16, 0:128].astype(F32) + wq_ref[0:16, 0:128].astype(F32)
    total = total + wkv_ref[0:16, 0:128].astype(F32) + wo_ref[0:16, 0:128].astype(F32)
    out_ref[...] = total


def own_first_kernel(own_ref, we_ref, wq_ref, wkv_ref, x0_ref, q_ref, kv_ref, x_s, n_s):
    means = group_mean_matrix()

    for g in range(GROUPS):
        x_s[:, cols(g)] = dot(own_ref[...], we_ref[:, cols(g)]).astype(BF).astype(F32)

    residual = x_s[...]
    n_s[...] = (residual * row_scale(residual)).astype(BF)
    x0_ref[...] = residual[32:288].astype(BF)

    for g in range(GROUPS):
        query = dot(n_s[32:288, :], wq_ref[:, cols(g)])
        query = query * lax.rsqrt(group_mean(query * query, means) + EPSILON)
        q_ref[:, cols(g)] = (query.astype(BF) * 0.125).astype(BF)
        key = dot(n_s[...], wkv_ref[:, cols(g)])
        key = key * lax.rsqrt(group_mean(key * key, means) + EPSILON)
        kv_ref[:, cols(g)] = key.astype(BF)
        kv_ref[:, cols(g + GROUPS)] = dot(n_s[...], wkv_ref[:, cols(g + GROUPS)]).astype(BF)


def keys_of(kv_ref, rim_ref, block, group):
    rim = rim_ref.shape[0] // 2
    lanes = cols(group)
    return jnp.concatenate(
        [
            kv_ref[64 * block : 64 * block + 128, lanes],
            rim_ref[32 * block : 32 * block + 64, lanes],
            rim_ref[rim + 32 * block : rim + 32 * block + 64, lanes],
        ],
        axis=0,
    )


def padded_rim(values):
    half = values.shape[0] // 2
    pad = jnp.zeros((8, values.shape[1]), F32)
    return jnp.concatenate([pad, values[:half], pad, pad, values[half:], pad], axis=0)


def first_core_kernel(
    grid_rows, grid_cols,
    place_ref, a_ref, b_ref, we_ref, wkv_ref, wo_ref, x0_ref, q_ref, kv_ref,
    x1_ref, go_a_ref, go_b_ref,
    p_s, x_s, n_s, rim_s, o_s, mask_s,
):
    means = group_mean_matrix()
    p_s[0:144, :] = a_ref[...]
    p_s[144:288, :] = b_ref[...]

    for g in range(GROUPS):
        x_s[:, cols(g)] = dot(p_s[...], we_ref[:, cols(g)]).astype(BF).astype(F32)

    residual = x_s[...]
    n_s[...] = (residual * row_scale(residual)).astype(BF)

    for g in range(GROUPS):
        key = dot(n_s[...], wkv_ref[:, cols(g)])
        key = key * lax.rsqrt(group_mean(key * key, means) + EPSILON)
        rim_s[:, cols(g)] = padded_rim(key).astype(BF)
        value = dot(n_s[...], wkv_ref[:, cols(g + GROUPS)])
        rim_s[:, cols(g + GROUPS)] = padded_rim(value).astype(BF)

    first_row = place_ref[0] * 16 - 12
    for block in range(4):
        mask_s[block] = block_mask(first_row + 8 * block, place_ref[1], grid_rows, grid_cols)
    masks = head_masks()

    for g in range(GROUPS):
        for block in range(4):
            query = stack_heads(q_ref[64 * block : 64 * block + 64, cols(g)], masks)
            key = keys_of(kv_ref, rim_s, block, g)
            value = keys_of(kv_ref, rim_s, block, g + GROUPS)
            weight, inverse = softmax_parts(dot(query, key, NT), mask_s[block])
            mixed = dot(weight.astype(BF), value) * inverse
            o_s[64 * block : 64 * block + 64, cols(g)] = unstack_heads(mixed).astype(BF)

    n = iota((112, 256), 0)
    edge = ((n >> 2) + 2) * 8 + (n & 3)
    source = iota((112, 256), 1)
    even = 1 - (place_ref[1] & 1)
    pick_a = jnp.where(edge + 4 * even == source, 1.0, 0.0).astype(BF)
    pick_b = jnp.where(edge + 4 * (1 - even) == source, 1.0, 0.0).astype(BF)

    for g in range(GROUPS):
        total = x0_ref[:, cols(g)].astype(F32) + dot(o_s[...], wo_ref[:, cols(g)])
        total = total.astype(BF)
        x1_ref[:, cols(g)] = total
        go_a_ref[:, cols(g)] = dot(pick_a, total).astype(BF)
        go_b_ref[:, cols(g)] = dot(pick_b, total).astype(BF)


def own_second_kernel(
    x1_ref, cot_ref, above_ref, below_ref, wq_ref, wkv_ref, wo_ref,
    q_ref, kv_ref, do_ref, rsq_ref, rsk_ref,
    n_s, c_s,
):
    means = group_mean_matrix()
    residual = x1_ref[...].astype(F32)
    n_s[...] = (residual * row_scale(residual)).astype(BF)
    c_s[0:32, :] = above_ref[...]
    c_s[32:160, :] = cot_ref[...]
    c_s[160:192, :] = below_ref[...]

    for g in range(GROUPS):
        query = dot(n_s[32:224, :], wq_ref[:, cols(g)])
        scale = lax.rsqrt(group_mean(query * query, means) + EPSILON)
        q_ref[:, cols(g)] = ((query * scale).astype(BF) * 0.125).astype(BF)
        rsq_ref[:, cols(g)] = scale[32:160]
        key = dot(n_s[...], wkv_ref[:, cols(g)])
        scale = lax.rsqrt(group_mean(key * key, means) + EPSILON)
        kv_ref[:, cols(g)] = (key * scale).astype(BF)
        rsk_ref[:, cols(g)] = scale[64:192]
        kv_ref[:, cols(g + GROUPS)] = dot(n_s[...], wkv_ref[:, cols(g + GROUPS)]).astype(BF)
        do_ref[:, cols(g)] = dot(c_s[...], wo_ref[cols(g), :], NT).astype(BF)


def head_scale_back(back, normed, scale, means):
    return scale * (back - normed * group_mean(back * normed, means))


def second_core_kernel(
    grid_rows, grid_cols,
    place_ref, a_ref, b_ref, wkv_ref, q_ref, kv_ref, do_ref,
    o_ref, dq_ref, dkv_ref, go_a_ref, go_b_ref,
    n_s, rim_s, rs_s, db_s, mask_s,
):
    means = group_mean_matrix()
    residual = jnp.concatenate([a_ref[...].astype(F32), b_ref[...].astype(F32)], axis=0)
    residual = padded_rim(residual)
    n_s[...] = (residual * row_scale(residual)).astype(BF)

    for g in range(GROUPS):
        key = dot(n_s[...], wkv_ref[:, cols(g)])
        scale = lax.rsqrt(group_mean(key * key, means) + EPSILON)
        rim_s[:, cols(g)] = (key * scale).astype(BF)
        rs_s[0:64, cols(g)] = scale[32:96]
        rs_s[64:128, cols(g)] = scale[160:224]
        rim_s[:, cols(g + GROUPS)] = dot(n_s[...], wkv_ref[:, cols(g + GROUPS)]).astype(BF)

    first_row = place_ref[0] * 16 - 8
    for block in range(3):
        mask_s[block] = block_mask(first_row + 8 * block, place_ref[1], grid_rows, grid_cols)
    masks = head_masks()

    for g in range(GROUPS):
        key_backs, value_backs = [], []
        for block in range(3):
            query = stack_heads(q_ref[64 * block : 64 * block + 64, cols(g)], masks)
            key = keys_of(kv_ref, rim_s, block, g)
            value = keys_of(kv_ref, rim_s, block, g + GROUPS)
            weight, inverse = softmax_parts(dot(query, key, NT), mask_s[block])
            probs = weight * inverse
            probs_low = probs.astype(BF)
            out_back = stack_heads(do_ref[64 * block : 64 * block + 64, cols(g)], masks)
            probs_back = dot(out_back, value, NT)
            centre = jnp.sum(probs_back * probs, axis=-1, keepdims=True)
            scores_back = (probs * (probs_back - centre)).astype(BF)
            o_ref[64 * block : 64 * block + 64, cols(g)] = unstack_heads(
                dot(probs_low, value)
            ).astype(BF)
            dq_ref[64 * block : 64 * block + 64, cols(g)] = unstack_heads(
                dot(scores_back, key)
            ).astype(BF)
            key_backs.append(dot(scores_back, query, TN))
            value_backs.append(dot(probs_low, out_back, TN))

        def fold(parts):
            def piece(start, half):
                return jnp.concatenate(
                    [
                        parts[0][start + half : start + 2 * half] + parts[1][start : start + half],
                        parts[1][start + half : start + 2 * half] + parts[2][start : start + half],
                    ],
                    axis=0,
                )

            return piece(0, 64), jnp.concatenate([piece(128, 32), piece(192, 32)], axis=0)

        own, rim = fold(key_backs)
        dkv_ref[:, cols(g)] = own.astype(BF)
        normed = jnp.concatenate([rim_s[32:96, cols(g)], rim_s[160:224, cols(g)]], axis=0)
        rim = head_scale_back(rim, normed.astype(F32), rs_s[:, cols(g)], means)
        db_s[:, cols(g)] = rim.astype(BF)
        own, rim = fold(value_backs)
        dkv_ref[:, cols(g + GROUPS)] = own.astype(BF)
        db_s[:, cols(g + GROUPS)] = rim.astype(BF)

    for g in range(GROUPS):
        back = dot(db_s[...], wkv_ref[cols(g), :], NT).astype(BF)
        go_a_ref[:, cols(g)] = back[:64]
        go_b_ref[:, cols(g)] = back[64:]


def own_back_kernel(
    x1_ref, o_ref, dq_ref, dkv_ref, q_ref, kv_ref, rsq_ref, rsk_ref, wq_ref, wkv_ref, wo_ref,
    out_ref, dn_ref,
    a_s, b_s,
):
    means = group_mean_matrix()

    for g in range(GROUPS):
        total = x1_ref[64:192, cols(g)].astype(F32) + dot(o_ref[32:160, :], wo_ref[:, cols(g)])
        out_ref[:, cols(g)] = total.astype(BF)
        back = dq_ref[32:160, cols(g)].astype(F32) * 0.125
        normed = q_ref[32:160, cols(g)].astype(F32) * 8.0
        a_s[:, cols(g)] = head_scale_back(back, normed, rsq_ref[:, cols(g)], means).astype(BF)
        back = dkv_ref[:, cols(g)].astype(F32)
        normed = kv_ref[64:192, cols(g)].astype(F32)
        b_s[:, cols(g)] = head_scale_back(back, normed, rsk_ref[:, cols(g)], means).astype(BF)
        b_s[:, cols(g + GROUPS)] = dkv_ref[:, cols(g + GROUPS)]

    for g in range(GROUPS):
        back = dot(a_s[...], wq_ref[cols(g), :], NT) + dot(b_s[...], wkv_ref[cols(g), :], NT)
        dn_ref[:, cols(g)] = back


def last_kernel(place_ref, x1_ref, cot_ref, dn_ref, a_ref, b_ref, out_ref):
    n, source = iota((128, 128), 0), iota((128, 128), 1)
    right = (source < 64) == ((place_ref[1] & 1) == 0)
    column = jnp.where(right, (source & 3) + 4, source & 3)
    token = ((source & 63) >> 2) * 8 + column
    pick = jnp.where(n == token, 1.0, 0.0).astype(BF)
    arrived = jnp.concatenate([a_ref[...], b_ref[...]], axis=0)
    back = dn_ref[...] + dot(pick, arrived)
    residual = x1_ref[64:192, :].astype(F32)
    scale = row_scale(residual)
    normed = residual * scale
    mean = jnp.mean(back * normed, axis=-1, keepdims=True)
    out_ref[...] = (cot_ref[...].astype(F32) + scale * (back - normed * mean)).astype(BF)


def call(kernel, out_shapes, *operands, scratch=(), flops=0, moved=0, small=None, hbm=False):
    vmem = pl.BlockSpec(memory_space=pltpu.VMEM)
    in_specs = [pl.BlockSpec(memory_space=pltpu.HBM) if hbm else vmem] * len(operands)
    if small is not None:
        operands = (small,) + operands
        in_specs = [pl.BlockSpec(memory_space=pltpu.SMEM)] + in_specs
    shapes = tuple(jax.ShapeDtypeStruct(s, d) for s, d in out_shapes)
    return pl.pallas_call(
        kernel,
        out_shape=shapes,
        in_specs=in_specs,
        out_specs=tuple(vmem for _ in shapes),
        scratch_shapes=[s if d is None else pltpu.VMEM(s, d) for s, d in scratch],
        compiler_params=pltpu.CompilerParams(vmem_limit_bytes=32 * 1024 * 1024),
        cost_estimate=pl.CostEstimate(flops=flops, bytes_accessed=moved, transcendentals=0),
    )(*operands)


def shift(values, axis, step):
    peers = lax.axis_size(axis)
    return lax.ppermute(
        values, axis, [(i, i + step) for i in range(peers) if 0 <= i + step < peers]
    )


def trade(values, axis, step):
    return lax.ppermute(values, axis, [(i, i ^ step) for i in range(lax.axis_size(axis))])


def trade_sides(go_a, go_b):
    peers = lax.axis_size("col")
    across = [(i, ((i + 1) ^ 1) - 1) for i in range(peers)]
    b = lax.ppermute(go_b, "col", [(i, j) for i, j in across if 0 <= j < peers])
    return trade(go_a, "col", 1), b


def on_device(patches, tile_slot, w_embed, w_query, w_keyval, w_out, cotangent):
    rows, columns = lax.axis_size("row"), lax.axis_size("col")
    grid_rows, grid_cols = rows * 16, columns * 8
    place = jnp.stack([lax.axis_index("row"), lax.axis_index("col")]).astype(jnp.int32)
    cot = cotangent.reshape(128, D)
    window = ((96, PIX + 128), BF)

    own, far = call(
        pack_kernel, (window, window), patches, tile_slot.reshape(1, 128),
        small=place, hbm=True,
        scratch=(
            ((1, 128), jnp.int32), ((128, 128), BF), (pltpu.SemaphoreType.DMA((3,)), None)
        ),
    )
    far = trade(far, "row", 4)
    (touched,) = call(
        touch_kernel, (((16, 128), F32),), w_embed, w_query, w_keyval, w_out
    )
    sends = call(spread_kernel, (window, window, window), own, far, touched, small=place)
    arrived = [trade(send, "row", step) for send, step in zip(sends, (2, 3, 1))]

    above = shift(cot[96:], "row", 1)
    below = shift(cot[:32], "row", -1)

    own, go_a, go_b = call(
        place_kernel,
        (((320, PIX), BF), ((144, PIX), BF), ((144, PIX), BF)),
        own, far, *arrived,
        small=place,
    )
    a, b = trade_sides(go_a, go_b)
    x0, queries, keyval = call(
        own_first_kernel,
        (((256, D), BF), ((256, D), BF), ((320, 2 * D), BF)),
        own, w_embed, w_query, w_keyval,
        scratch=(((320, D), F32), ((320, D), BF)),
        flops=8 * 10**9, moved=8 * 10**6,
    )
    x1, go_a, go_b = call(
        functools.partial(first_core_kernel, grid_rows, grid_cols),
        (((256, D), BF), ((112, D), BF), ((112, D), BF)),
        a, b, w_embed, w_keyval, w_out, x0, queries, keyval,
        small=place,
        scratch=(
            ((288, PIX), BF), ((288, D), F32), ((288, D), BF), ((320, 2 * D), BF), ((256, D), BF),
            ((4, 256, 256), F32),
        ),
        flops=8 * 10**9, moved=8 * 10**6,
    )
    a, b = trade_sides(go_a, go_b)
    queries, keyval, out_back, query_scale, key_scale = call(
        own_second_kernel,
        (((192, D), BF), ((256, 2 * D), BF), ((192, D), BF), ((128, D), F32), ((128, D), F32)),
        x1, cot, above, below, w_query, w_keyval, w_out,
        scratch=(((256, D), BF), ((192, D), BF)),
        flops=8 * 10**9, moved=8 * 10**6,
    )
    attended, dq, dkv, go_a, go_b = call(
        functools.partial(second_core_kernel, grid_rows, grid_cols),
        (((192, D), BF), ((192, D), BF), ((128, 2 * D), BF), ((64, D), BF), ((64, D), BF)),
        a, b, w_keyval, queries, keyval, out_back,
        small=place,
        scratch=(
            ((256, D), BF), ((256, 2 * D), BF), ((128, D), F32), ((128, 2 * D), BF),
            ((3, 256, 256), F32),
        ),
        flops=8 * 10**9, moved=8 * 10**6,
    )
    a, b = trade_sides(go_a, go_b)
    final_tokens, back = call(
        own_back_kernel,
        (((128, D), BF), ((128, D), F32)),
        x1, attended, dq, dkv, queries, keyval, query_scale, key_scale, w_query, w_keyval, w_out,
        scratch=(((128, D), BF), ((128, 2 * D), BF)),
        flops=8 * 10**9, moved=8 * 10**6,
    )
    (input_grad,) = call(last_kernel, (((128, D), BF),), x1, cot, back, a, b, small=place)
    return final_tokens.reshape(16, 8, D), input_grad.reshape(16, 8, D)


def solution(mesh):
    in_specs = (
        P(("row", "col"), None),
        P(("row", "col")),
        P(),
        P(),
        P(),
        P(),
        P("row", "col", None),
    )
    out_specs = (P("row", "col", None), P("row", "col", None))
    return jax.shard_map(
        on_device, mesh=mesh, in_specs=in_specs, out_specs=out_specs, check_vma=False
    )
```

```python
import functools

import jax
import jax.numpy as jnp
from jax import lax
from jax.experimental import pallas as pl
from jax.experimental.pallas import tpu as pltpu
from jax.sharding import PartitionSpec as P

D = 1024
PIX = 768
EPSILON = 1e-06
F32 = jnp.float32
BF = jnp.bfloat16
LANES = 256
GROUPS = D // LANES
NT = (((1,), (1,)), ((), ()))
NN = (((1,), (0,)), ((), ()))
TN = (((0,), (0,)), ((), ()))


def dot(a, b, dims=NN):
    return lax.dot_general(a, b, dims, preferred_element_type=F32)


def iota(shape, axis):
    return lax.broadcasted_iota(jnp.int32, shape, axis)


def group_mean_matrix():
    same = (iota((LANES, LANES), 0) >> 6) == (iota((LANES, LANES), 1) >> 6)
    return jnp.where(same, 1.0 / 64, 0.0).astype(BF)


def group_mean(values, means):
    return dot(values.astype(BF), means)


def row_scale(residual):
    return lax.rsqrt(jnp.mean(residual * residual, axis=-1, keepdims=True) + EPSILON)


def cols(index):
    return slice(index * LANES, index * LANES + LANES)


def head_masks():
    lane = iota((1, LANES), 1) >> 6
    return [jnp.where(lane == h, 1.0, 0.0).astype(BF) for h in range(4)]


def stack_heads(values, masks):
    return jnp.concatenate([values * mask for mask in masks], axis=0)


def unstack_heads(stacked):
    lane = iota((64, LANES), 1) >> 6
    parts = [stacked[64 * h : 64 * h + 64] for h in range(4)]
    low = jnp.where(lane == 0, parts[0], parts[1])
    high = jnp.where(lane == 2, parts[2], parts[3])
    return jnp.where(lane < 2, low, high)


def key_places(key, first_row, col_index, grid_rows, grid_cols):
    right = (key < 192) == ((col_index & 1) == 0)
    rim = key & 63
    key_row = jnp.where(key < 128, key >> 3, rim >> 2)
    rim_col = jnp.where(right, (rim & 3) + 8, (rim & 3) - 4)
    key_col = jnp.where(key < 128, key & 7, rim_col)
    row = first_row + key_row
    col = col_index * 8 + key_col
    inside = (row >= 0) & (row < grid_rows) & (col >= 0) & (col < grid_cols)
    return key_row, key_col, jnp.where(inside, 1.0, 0.0)


def block_masks(axis, first_row, blocks, col_index, grid_rows, grid_cols):
    shapes = (256, 1), (1, 256)
    key, token = iota(shapes[axis], axis), iota(shapes[1 - axis], 1 - axis) & 63
    for block in range(blocks):
        key_row, key_col, inside = key_places(
            key, first_row + 8 * block, col_index, grid_rows, grid_cols
        )
        if block == 0:
            row_gap = key_row - (token >> 3) - 4
            col_gap = key_col - (token & 7)
            near = (row_gap >= -3) & (row_gap <= 3) & (col_gap >= -3) & (col_gap <= 3)
            near = jnp.where(near, 1.0, 0.0)
        yield near * inside


def column_softmax(scores, mask):
    weight = jnp.exp(scores) * mask
    total = jnp.sum(weight, axis=0, keepdims=True)
    return weight * (1.0 / jnp.where(total > 0, total, 1.0))


def pack_kernel(
    place_ref, patches_ref, slot_ref, cot_ref,
    own_ref, far_ref, go_c_ref, go_d_ref, slot_s, wide_s, sems,
):
    half = place_ref[0] >> 2
    odd = place_ref[0] & 1
    own_rows = pl.ds(pl.multiple_of(16 - 16 * half, 16), 80)
    own_source = pl.ds(pl.multiple_of(48 * half, 16), 80)
    far_source = pl.ds(pl.multiple_of(48 - 48 * half, 16), 80)
    c_rows = pl.ds(pl.multiple_of(96 - 96 * odd, 16), 32)
    d_rows = pl.ds(pl.multiple_of(96 * odd, 16), 32)
    lanes = pl.ds(0, PIX)
    pairs = (
        (slot_ref, slot_s),
        (patches_ref.at[far_source, :], far_ref.at[:, lanes]),
        (patches_ref.at[own_source, :], own_ref.at[own_rows, lanes]),
        (cot_ref.at[c_rows, :], go_c_ref),
        (cot_ref.at[d_rows, :], go_d_ref),
    )
    copies = [pltpu.make_async_copy(*pair, sems.at[i]) for i, pair in enumerate(pairs)]
    for copy in copies:
        copy.start()
    for copy in copies:
        copy.wait()
    wide_s[...] = jnp.broadcast_to(slot_s[...].astype(F32), (128, 128)).T.astype(BF)
    gap = pl.ds(pl.multiple_of(80 * half, 16), 16)
    own_ref[gap, :] = jnp.zeros((16, PIX + 128), BF)
    own_ref[own_rows, PIX:] = wide_s[own_source, :]
    far_ref[:, PIX:] = wide_s[far_source, :]


def far_window(place_ref, far_ref, wide_ref):
    half = place_ref[0] >> 2
    wide_ref[pl.ds(pl.multiple_of(80 * half, 16), 16), :] = jnp.zeros((16, PIX + 128), BF)
    wide_ref[pl.ds(pl.multiple_of(16 - 16 * half, 16), 80), :] = far_ref[...]


def windows(place_ref, own_ref, far_ref, step):
    start = pl.multiple_of(((place_ref[0] & 3) ^ step) * 16, 16)
    return own_ref[pl.ds(start, 48), :], far_ref[pl.ds(start, 48), :]


def spread_kernel(
    place_ref, own_ref, far_ref, mask_a_ref, mask_b_ref, *refs
):
    far_s = refs[3]
    far_window(place_ref, far_ref, far_s)
    for step, out_ref in zip((2, 3, 1), refs):
        near, far = windows(place_ref, own_ref, far_s, step)
        out_ref[0:48, :] = near
        out_ref[48:96, :] = far


def place_kernel(
    place_ref, touched_ref, own_in_ref, far_in_ref, in2_ref, in3_ref, in1_ref,
    own_ref, go_a_ref, go_b_ref, far_s,
):
    far_window(place_ref, far_in_ref, far_s)
    near, far = windows(place_ref, own_in_ref, far_s, 0)
    source = jnp.concatenate([near, far, in2_ref[...], in3_ref[...], in1_ref[...]], axis=0)
    slots = []
    for part in range(3):
        slots.append(source[128 * part : 128 * part + 128, PIX:].astype(F32).T[:8])
    tile = lax.rem(iota((8, 384), 1) >> 4, 3)
    slot = jnp.concatenate(slots, axis=1) + 128.0 * tile.astype(F32)
    source = source[:, :PIX]
    even = 1 - (place_ref[1] & 1)

    def pick(position):
        hot = jnp.where(position.astype(F32) == slot[:1], 1.0, 0.0).astype(BF)
        return dot(hot, source).astype(BF)

    own_ref[...] = pick(iota((320, 384), 0) + 32)
    n = iota((144, 384), 0)
    edge = ((n >> 2) + 6) * 8 + (n & 3)
    go_a_ref[...] = pick(edge + 4 * even)
    go_b_ref[...] = pick(edge + 4 * (1 - even))


def mask_kernel(grid_rows, grid_cols, place_ref, wkv_ref, first_ref, second_ref):
    row, col = place_ref[0] * 16, place_ref[1]
    for i, mask in enumerate(block_masks(1, row - 12, 4, col, grid_rows, grid_cols)):
        first_ref[i] = mask
    for i, mask in enumerate(block_masks(0, row - 8, 3, col, grid_rows, grid_cols)):
        second_ref[i] = mask


def touch_kernel(we_ref, wq_ref, send_ref, out_ref):
    out_ref[...] = we_ref[0:16, 0:128].astype(F32) + wq_ref[0:16, 0:128].astype(F32)


def own_first_kernel(own_ref, we_ref, wq_ref, wkv_ref, x0_ref, q_ref, kv_ref, x_s, n_s):
    means = group_mean_matrix()

    for g in range(GROUPS):
        x_s[:, cols(g)] = dot(own_ref[...], we_ref[:, cols(g)]).astype(BF).astype(F32)

    residual = x_s[...]
    n_s[...] = (residual * row_scale(residual)).astype(BF)
    x0_ref[...] = residual[32:288].astype(BF)

    for g in range(GROUPS):
        query = dot(n_s[32:288, :], wq_ref[:, cols(g)])
        query = query * lax.rsqrt(group_mean(query * query, means) + EPSILON)
        q_ref[:, cols(g)] = (query.astype(BF) * 0.125).astype(BF)
        key = dot(n_s[...], wkv_ref[:, cols(g)])
        key = key * lax.rsqrt(group_mean(key * key, means) + EPSILON)
        kv_ref[:, cols(g)] = key.astype(BF)
        kv_ref[:, cols(g + GROUPS)] = dot(n_s[...], wkv_ref[:, cols(g + GROUPS)]).astype(BF)


def keys_of(kv_ref, rim_ref, block, group):
    rim = rim_ref.shape[0] // 2
    lanes = cols(group)
    return jnp.concatenate(
        [
            kv_ref[64 * block : 64 * block + 128, lanes],
            rim_ref[32 * block : 32 * block + 64, lanes],
            rim_ref[rim + 32 * block : rim + 32 * block + 64, lanes],
        ],
        axis=0,
    )


def padded_rim(values):
    half = values.shape[0] // 2
    pad = jnp.zeros((8, values.shape[1]), F32)
    return jnp.concatenate([pad, values[:half], pad, pad, values[half:], pad], axis=0)


def first_core_kernel(
    place_ref, mask_ref, a_ref, b_ref, we_ref, wkv_ref, wo_ref, x0_ref, q_ref, kv_ref,
    x1_ref, go_a_ref, go_b_ref,
    p_s, x_s, n_s, rim_s, o_s,
):
    means = group_mean_matrix()
    p_s[0:144, :] = a_ref[...]
    p_s[144:288, :] = b_ref[...]

    for g in range(GROUPS):
        x_s[:, cols(g)] = dot(p_s[...], we_ref[:, cols(g)]).astype(BF).astype(F32)

    residual = x_s[...]
    n_s[...] = (residual * row_scale(residual)).astype(BF)

    for g in range(GROUPS):
        key = dot(n_s[...], wkv_ref[:, cols(g)])
        key = key * lax.rsqrt(group_mean(key * key, means) + EPSILON)
        rim_s[:, cols(g)] = padded_rim(key).astype(BF)
        value = dot(n_s[...], wkv_ref[:, cols(g + GROUPS)])
        rim_s[:, cols(g + GROUPS)] = padded_rim(value).astype(BF)

    masks = head_masks()

    for g in range(GROUPS):
        for block in range(4):
            query = stack_heads(q_ref[64 * block : 64 * block + 64, cols(g)], masks)
            key = keys_of(kv_ref, rim_s, block, g)
            value = keys_of(kv_ref, rim_s, block, g + GROUPS)
            weight = jnp.exp(dot(query, key, NT)) * mask_ref[block]
            total = jnp.sum(weight, axis=1, keepdims=True)
            mixed = dot(weight.astype(BF), value) * (1.0 / jnp.where(total > 0, total, 1.0))
            o_s[64 * block : 64 * block + 64, cols(g)] = unstack_heads(mixed).astype(BF)

    n = iota((112, 256), 0)
    edge = ((n >> 2) + 2) * 8 + (n & 3)
    source = iota((112, 256), 1)
    even = 1 - (place_ref[1] & 1)
    pick_a = jnp.where(edge + 4 * even == source, 1.0, 0.0).astype(BF)
    pick_b = jnp.where(edge + 4 * (1 - even) == source, 1.0, 0.0).astype(BF)

    for g in range(GROUPS):
        total = x0_ref[:, cols(g)].astype(F32) + dot(o_s[...], wo_ref[:, cols(g)])
        total = total.astype(BF)
        x1_ref[:, cols(g)] = total
        go_a_ref[:, cols(g)] = dot(pick_a, total).astype(BF)
        go_b_ref[:, cols(g)] = dot(pick_b, total).astype(BF)


def own_second_kernel(
    place_ref, x1_ref, cot_ref, c_ref, d_ref, wq_ref, wkv_ref, wo_ref,
    q_ref, kv_ref, do_ref, rsq_ref, rsk_ref,
    n_s, c_s,
):
    means = group_mean_matrix()
    residual = x1_ref[...].astype(F32)
    n_s[...] = (residual * row_scale(residual)).astype(BF)
    odd = place_ref[0] & 1
    c_s[pl.ds(pl.multiple_of(160 - 160 * odd, 16), 32), :] = c_ref[...]
    c_s[32:160, :] = cot_ref[...]
    c_s[pl.ds(pl.multiple_of(160 * odd, 16), 32), :] = d_ref[...]

    for g in range(GROUPS):
        query = dot(n_s[32:224, :], wq_ref[:, cols(g)])
        scale = lax.rsqrt(group_mean(query * query, means) + EPSILON)
        q_ref[:, cols(g)] = ((query * scale).astype(BF) * 0.125).astype(BF)
        rsq_ref[:, cols(g)] = scale[32:160]
        key = dot(n_s[...], wkv_ref[:, cols(g)])
        scale = lax.rsqrt(group_mean(key * key, means) + EPSILON)
        kv_ref[:, cols(g)] = (key * scale).astype(BF)
        rsk_ref[:, cols(g)] = scale[64:192]
        kv_ref[:, cols(g + GROUPS)] = dot(n_s[...], wkv_ref[:, cols(g + GROUPS)]).astype(BF)
        do_ref[:, cols(g)] = dot(c_s[...], wo_ref[cols(g), :], NT).astype(BF)


def head_scale_back(back, normed, scale, means):
    return scale * (back - normed * group_mean(back * normed, means))


def second_core_kernel(
    mask_ref, a_ref, b_ref, wkv_ref, q_ref, kv_ref, do_ref,
    o_ref, dq_ref, dkv_ref, go_a_ref, go_b_ref,
    n_s, rim_s, rs_s, db_s,
):
    means = group_mean_matrix()
    residual = jnp.concatenate([a_ref[...].astype(F32), b_ref[...].astype(F32)], axis=0)
    residual = padded_rim(residual)
    n_s[...] = (residual * row_scale(residual)).astype(BF)

    for g in range(GROUPS):
        key = dot(n_s[...], wkv_ref[:, cols(g)])
        scale = lax.rsqrt(group_mean(key * key, means) + EPSILON)
        rim_s[:, cols(g)] = (key * scale).astype(BF)
        rs_s[0:64, cols(g)] = scale[32:96]
        rs_s[64:128, cols(g)] = scale[160:224]
        rim_s[:, cols(g + GROUPS)] = dot(n_s[...], wkv_ref[:, cols(g + GROUPS)]).astype(BF)

    masks = head_masks()

    for g in range(GROUPS):
        key_backs, value_backs = [], []
        for block in range(3):
            query = stack_heads(q_ref[64 * block : 64 * block + 64, cols(g)], masks)
            key = keys_of(kv_ref, rim_s, block, g)
            value = keys_of(kv_ref, rim_s, block, g + GROUPS)
            out_back = stack_heads(do_ref[64 * block : 64 * block + 64, cols(g)], masks)
            probs = column_softmax(dot(key, query, NT), mask_ref[block])
            probs_low = probs.astype(BF)
            probs_back = dot(value, out_back, NT)
            centre = jnp.sum(probs_back * probs, axis=0, keepdims=True)
            scores_back = (probs * (probs_back - centre)).astype(BF)
            o_ref[64 * block : 64 * block + 64, cols(g)] = unstack_heads(
                dot(probs_low, value, TN)
            ).astype(BF)
            dq_ref[64 * block : 64 * block + 64, cols(g)] = unstack_heads(
                dot(scores_back, key, TN)
            ).astype(BF)
            key_backs.append(dot(scores_back, query))
            value_backs.append(dot(probs_low, out_back))

        def fold(parts):
            def piece(start, half):
                return jnp.concatenate(
                    [
                        parts[0][start + half : start + 2 * half] + parts[1][start : start + half],
                        parts[1][start + half : start + 2 * half] + parts[2][start : start + half],
                    ],
                    axis=0,
                )

            return piece(0, 64), jnp.concatenate([piece(128, 32), piece(192, 32)], axis=0)

        own, rim = fold(key_backs)
        dkv_ref[:, cols(g)] = own.astype(BF)
        normed = jnp.concatenate([rim_s[32:96, cols(g)], rim_s[160:224, cols(g)]], axis=0)
        rim = head_scale_back(rim, normed.astype(F32), rs_s[:, cols(g)], means)
        db_s[:, cols(g)] = rim.astype(BF)
        own, rim = fold(value_backs)
        dkv_ref[:, cols(g + GROUPS)] = own.astype(BF)
        db_s[:, cols(g + GROUPS)] = rim.astype(BF)

    for g in range(GROUPS):
        back = dot(db_s[...], wkv_ref[cols(g), :], NT).astype(BF)
        go_a_ref[:, cols(g)] = back[:64]
        go_b_ref[:, cols(g)] = back[64:]


def own_back_kernel(
    x1_ref, o_ref, dq_ref, dkv_ref, q_ref, kv_ref, rsq_ref, rsk_ref, wq_ref, wkv_ref, wo_ref,
    out_ref, dn_ref,
    a_s, b_s,
):
    means = group_mean_matrix()

    for g in range(GROUPS):
        total = x1_ref[64:192, cols(g)].astype(F32) + dot(o_ref[32:160, :], wo_ref[:, cols(g)])
        out_ref[:, cols(g)] = total.astype(BF)
        back = dq_ref[32:160, cols(g)].astype(F32) * 0.125
        normed = q_ref[32:160, cols(g)].astype(F32) * 8.0
        a_s[:, cols(g)] = head_scale_back(back, normed, rsq_ref[:, cols(g)], means).astype(BF)
        back = dkv_ref[:, cols(g)].astype(F32)
        normed = kv_ref[64:192, cols(g)].astype(F32)
        b_s[:, cols(g)] = head_scale_back(back, normed, rsk_ref[:, cols(g)], means).astype(BF)
        b_s[:, cols(g + GROUPS)] = dkv_ref[:, cols(g + GROUPS)]

    for g in range(GROUPS):
        back = dot(a_s[...], wq_ref[cols(g), :], NT) + dot(b_s[...], wkv_ref[cols(g), :], NT)
        dn_ref[:, cols(g)] = back


def last_kernel(place_ref, x1_ref, cot_ref, dn_ref, a_ref, b_ref, out_ref):
    n, source = iota((128, 128), 0), iota((128, 128), 1)
    right = (source < 64) == ((place_ref[1] & 1) == 0)
    column = jnp.where(right, (source & 3) + 4, source & 3)
    token = ((source & 63) >> 2) * 8 + column
    pick = jnp.where(n == token, 1.0, 0.0).astype(BF)
    arrived = jnp.concatenate([a_ref[...], b_ref[...]], axis=0)
    back = dn_ref[...] + dot(pick, arrived)
    residual = x1_ref[64:192, :].astype(F32)
    scale = row_scale(residual)
    normed = residual * scale
    mean = jnp.mean(back * normed, axis=-1, keepdims=True)
    out_ref[...] = (cot_ref[...].astype(F32) + scale * (back - normed * mean)).astype(BF)


def call(kernel, out_shapes, *operands, scratch=(), flops=0, moved=0, small=None, hbm=False):
    vmem = pl.BlockSpec(memory_space=pltpu.VMEM)
    in_specs = [pl.BlockSpec(memory_space=pltpu.HBM) if hbm else vmem] * len(operands)
    if hbm:
        operands = tuple(pltpu.with_memory_space_constraint(x, pltpu.HBM) for x in operands)
    if small is not None:
        operands = (small,) + operands
        in_specs = [pl.BlockSpec(memory_space=pltpu.SMEM)] + in_specs
    shapes = tuple(jax.ShapeDtypeStruct(s, d) for s, d in out_shapes)
    return pl.pallas_call(
        kernel,
        out_shape=shapes,
        in_specs=in_specs,
        out_specs=tuple(vmem for _ in shapes),
        scratch_shapes=[s if d is None else pltpu.VMEM(s, d) for s, d in scratch],
        compiler_params=pltpu.CompilerParams(vmem_limit_bytes=32 * 1024 * 1024),
        cost_estimate=pl.CostEstimate(flops=flops, bytes_accessed=moved, transcendentals=0),
    )(*operands)


def trade(values, axis, step):
    return lax.ppermute(values, axis, [(i, i ^ step) for i in range(lax.axis_size(axis))])


def trade_sides(go_a, go_b, axis):
    peers = lax.axis_size(axis)
    across = [(i, ((i + 1) ^ 1) - 1) for i in range(peers)]
    b = lax.ppermute(go_b, axis, [(i, j) for i, j in across if 0 <= j < peers])
    return trade(go_a, axis, 1), b


def on_device(patches, tile_slot, w_embed, w_query, w_keyval, w_out, cotangent):
    rows, columns = lax.axis_size("row"), lax.axis_size("col")
    grid_rows, grid_cols = rows * 16, columns * 8
    place = jnp.stack([lax.axis_index("row"), lax.axis_index("col")]).astype(jnp.int32)
    cot = cotangent.reshape(128, D)
    window = ((96, PIX + 128), BF)

    own, far, edge_c, edge_d = call(
        pack_kernel,
        (window, ((80, PIX + 128), BF), ((32, D), BF), ((32, D), BF)),
        patches, tile_slot.reshape(1, 128), cot,
        small=place, hbm=True,
        scratch=(
            ((1, 128), jnp.int32), ((128, 128), BF), (pltpu.SemaphoreType.DMA((5,)), None)
        ),
    )
    far = trade(far, "row", 4)
    masks = call(
        functools.partial(mask_kernel, grid_rows, grid_cols),
        (((4, 256, 256), F32), ((3, 256, 256), F32)),
        w_keyval,
        small=place,
    )
    sends = call(
        spread_kernel, (window, window, window), own, far, *masks,
        small=place, scratch=(window,),
    )
    (touched,) = call(touch_kernel, (((16, 128), F32),), w_embed, w_query, sends[0])
    arrived = [trade(send, "row", step) for send, step in zip(sends, (2, 3, 1))]
    edge_c, edge_d = trade_sides(edge_c, edge_d, "row")
    own, go_a, go_b = call(
        place_kernel,
        (((320, PIX), BF), ((144, PIX), BF), ((144, PIX), BF)),
        touched, own, far, *arrived,
        small=place,
        scratch=(window,),
    )
    a, b = trade_sides(go_a, go_b, "col")
    x0, queries, keyval = call(
        own_first_kernel,
        (((256, D), BF), ((256, D), BF), ((320, 2 * D), BF)),
        own, w_embed, w_query, w_keyval,
        scratch=(((320, D), F32), ((320, D), BF)),
        flops=8 * 10**9, moved=8 * 10**6,
    )
    x1, go_a, go_b = call(
        first_core_kernel,
        (((256, D), BF), ((112, D), BF), ((112, D), BF)),
        masks[0], a, b, w_embed, w_keyval, w_out, x0, queries, keyval,
        small=place,
        scratch=(
            ((288, PIX), BF), ((288, D), F32), ((288, D), BF), ((320, 2 * D), BF), ((256, D), BF),
        ),
        flops=8 * 10**9, moved=8 * 10**6,
    )
    a, b = trade_sides(go_a, go_b, "col")
    queries, keyval, out_back, query_scale, key_scale = call(
        own_second_kernel,
        (((192, D), BF), ((256, 2 * D), BF), ((192, D), BF), ((128, D), F32), ((128, D), F32)),
        x1, cot, edge_c, edge_d, w_query, w_keyval, w_out,
        small=place,
        scratch=(((256, D), BF), ((192, D), BF)),
        flops=8 * 10**9, moved=8 * 10**6,
    )
    attended, dq, dkv, go_a, go_b = call(
        second_core_kernel,
        (((192, D), BF), ((192, D), BF), ((128, 2 * D), BF), ((64, D), BF), ((64, D), BF)),
        masks[1], a, b, w_keyval, queries, keyval, out_back,
        scratch=(
            ((256, D), BF), ((256, 2 * D), BF), ((128, D), F32), ((128, 2 * D), BF),
        ),
        flops=8 * 10**9, moved=8 * 10**6,
    )
    a, b = trade_sides(go_a, go_b, "col")
    final_tokens, back = call(
        own_back_kernel,
        (((128, D), BF), ((128, D), F32)),
        x1, attended, dq, dkv, queries, keyval, query_scale, key_scale, w_query, w_keyval, w_out,
        scratch=(((128, D), BF), ((128, 2 * D), BF)),
        flops=8 * 10**9, moved=8 * 10**6,
    )
    (input_grad,) = call(last_kernel, (((128, D), BF),), x1, cot, back, a, b, small=place)
    return final_tokens.reshape(16, 8, D), input_grad.reshape(16, 8, D)


def solution(mesh):
    in_specs = (
        P(("row", "col"), None),
        P(("row", "col")),
        P(),
        P(),
        P(),
        P(),
        P("row", "col", None),
    )
    out_specs = (P("row", "col", None), P("row", "col", None))
    return jax.shard_map(
        on_device, mesh=mesh, in_specs=in_specs, out_specs=out_specs, check_vma=False
    )
```

```python
import functools

import jax
import jax.numpy as jnp
from jax import lax
from jax.experimental import pallas as pl
from jax.experimental.pallas import tpu as pltpu
from jax.sharding import PartitionSpec as P

D = 1024
PIX = 768
EPSILON = 1e-06
F32 = jnp.float32
BF = jnp.bfloat16
LANES = 256
GROUPS = D // LANES
NT = (((1,), (1,)), ((), ()))
NN = (((1,), (0,)), ((), ()))
TN = (((0,), (0,)), ((), ()))


def dot(a, b, dims=NN):
    return lax.dot_general(a, b, dims, preferred_element_type=F32)


def iota(shape, axis):
    return lax.broadcasted_iota(jnp.int32, shape, axis)


def group_mean_matrix():
    same = (iota((LANES, LANES), 0) >> 6) == (iota((LANES, LANES), 1) >> 6)
    return jnp.where(same, 1.0 / 64, 0.0).astype(BF)


def group_mean(values, means):
    return dot(values.astype(BF), means)


def row_scale(residual):
    return lax.rsqrt(jnp.mean(residual * residual, axis=-1, keepdims=True) + EPSILON)


def cols(index):
    return slice(index * LANES, index * LANES + LANES)


def head_masks():
    lane = iota((1, LANES), 1) >> 6
    return [jnp.where(lane == h, 1.0, 0.0).astype(BF) for h in range(4)]


def stack_heads(values, masks):
    return jnp.concatenate([values * mask for mask in masks], axis=0)


def unstack_heads(stacked):
    lane = iota((64, LANES), 1) >> 6
    parts = [stacked[64 * h : 64 * h + 64] for h in range(4)]
    low = jnp.where(lane == 0, parts[0], parts[1])
    high = jnp.where(lane == 2, parts[2], parts[3])
    return jnp.where(lane < 2, low, high)


def key_places(key, first_row, col_index, grid_rows, grid_cols):
    right = (key < 192) == ((col_index & 1) == 0)
    rim = key & 63
    key_row = jnp.where(key < 128, key >> 3, rim >> 2)
    rim_col = jnp.where(right, (rim & 3) + 8, (rim & 3) - 4)
    key_col = jnp.where(key < 128, key & 7, rim_col)
    row = first_row + key_row
    col = col_index * 8 + key_col
    inside = (row >= 0) & (row < grid_rows) & (col >= 0) & (col < grid_cols)
    return key_row, key_col, jnp.where(inside, 1.0, 0.0)


def block_masks(axis, first_row, blocks, col_index, grid_rows, grid_cols):
    shapes = (256, 1), (1, 256)
    key, token = iota(shapes[axis], axis), iota(shapes[1 - axis], 1 - axis) & 63
    for block in range(blocks):
        key_row, key_col, inside = key_places(
            key, first_row + 8 * block, col_index, grid_rows, grid_cols
        )
        if block == 0:
            row_gap = key_row - (token >> 3) - 4
            col_gap = key_col - (token & 7)
            near = (row_gap >= -3) & (row_gap <= 3) & (col_gap >= -3) & (col_gap <= 3)
            near = jnp.where(near, 1.0, 0.0)
        yield near * inside


def third(n):
    return (n * 171) >> 9


def edge_token(n, right):
    row = third(n)
    return row * 8 + (n - 3 * row) + 5 * right


def widen(shape, skipped, right):
    m, n = iota(shape, 0), iota(shape, 1)
    slot = (m & 3) - (1 - right)
    match = (((m >> 2) - skipped) * 3 + slot == n) & (slot >= 0) & (slot <= 2)
    return jnp.where(match, 1.0, 0.0).astype(BF)


def column_softmax(scores, mask):
    weight = jnp.exp(scores) * mask
    total = jnp.sum(weight, axis=0, keepdims=True)
    return weight * (1.0 / jnp.where(total > 0, total, 1.0))


def pack_kernel(
    place_ref, patches_ref, slot_ref, cot_ref,
    own_ref, far_ref, go_c_ref, go_d_ref, slot_s, wide_s, sems,
):
    half = place_ref[0] >> 2
    odd = place_ref[0] & 1
    own_rows = pl.ds(pl.multiple_of(16 - 16 * half, 16), 80)
    own_source = pl.ds(pl.multiple_of(48 * half, 16), 80)
    far_source = pl.ds(pl.multiple_of(48 - 48 * half, 16), 80)
    c_rows = pl.ds(pl.multiple_of(96 - 96 * odd, 16), 32)
    d_rows = pl.ds(pl.multiple_of(96 * odd, 16), 32)
    lanes = pl.ds(0, PIX)
    pairs = (
        (slot_ref, slot_s),
        (patches_ref.at[far_source, :], far_ref.at[:, lanes]),
        (patches_ref.at[own_source, :], own_ref.at[own_rows, lanes]),
        (cot_ref.at[c_rows, :], go_c_ref),
        (cot_ref.at[d_rows, :], go_d_ref),
    )
    copies = [pltpu.make_async_copy(*pair, sems.at[i]) for i, pair in enumerate(pairs)]
    for copy in copies:
        copy.start()
    for copy in copies:
        copy.wait()
    wide_s[...] = jnp.broadcast_to(slot_s[...].astype(F32), (128, 128)).T.astype(BF)
    gap = pl.ds(pl.multiple_of(80 * half, 16), 16)
    own_ref[gap, :] = jnp.zeros((16, PIX + 128), BF)
    own_ref[own_rows, PIX:] = wide_s[own_source, :]
    far_ref[:, PIX:] = wide_s[far_source, :]


def far_window(place_ref, far_ref, wide_ref):
    half = place_ref[0] >> 2
    wide_ref[pl.ds(pl.multiple_of(80 * half, 16), 16), :] = jnp.zeros((16, PIX + 128), BF)
    wide_ref[pl.ds(pl.multiple_of(16 - 16 * half, 16), 80), :] = far_ref[...]


def windows(place_ref, own_ref, far_ref, step):
    start = pl.multiple_of(((place_ref[0] & 3) ^ step) * 16, 16)
    return own_ref[pl.ds(start, 48), :], far_ref[pl.ds(start, 48), :]


def spread_kernel(
    place_ref, own_ref, far_ref, mask_a_ref, mask_b_ref, *refs
):
    far_s = refs[3]
    far_window(place_ref, far_ref, far_s)
    for step, out_ref in zip((2, 3, 1), refs):
        near, far = windows(place_ref, own_ref, far_s, step)
        out_ref[0:48, :] = near
        out_ref[48:96, :] = far


def place_kernel(
    place_ref, touched_ref, own_in_ref, far_in_ref, in2_ref, in3_ref, in1_ref,
    own_ref, go_a_ref, go_b_ref, far_s,
):
    far_window(place_ref, far_in_ref, far_s)
    near, far = windows(place_ref, own_in_ref, far_s, 0)
    source = jnp.concatenate([near, far, in2_ref[...], in3_ref[...], in1_ref[...]], axis=0)
    slots = []
    for part in range(3):
        slots.append(source[128 * part : 128 * part + 128, PIX:].astype(F32).T[:8])
    tile = lax.rem(iota((8, 384), 1) >> 4, 3)
    slot = jnp.concatenate(slots, axis=1) + 128.0 * tile.astype(F32)
    source = source[:, :PIX]
    even = 1 - (place_ref[1] & 1)

    def pick(position):
        hot = jnp.where(position.astype(F32) == slot[:1], 1.0, 0.0).astype(BF)
        return dot(hot, source).astype(BF)

    own_ref[...] = pick(iota((320, 384), 0) + 32)
    n = iota((112, 384), 0)
    go_a_ref[...] = pick(edge_token(n, even) + 48)
    go_b_ref[...] = pick(edge_token(n, 1 - even) + 48)


def mask_kernel(grid_rows, grid_cols, place_ref, wkv_ref, first_ref, second_ref):
    row, col = place_ref[0] * 16, place_ref[1]
    for i, mask in enumerate(block_masks(1, row - 12, 4, col, grid_rows, grid_cols)):
        first_ref[i] = mask
    for i, mask in enumerate(block_masks(0, row - 8, 3, col, grid_rows, grid_cols)):
        second_ref[i] = mask


def touch_kernel(we_ref, wq_ref, send_ref, out_ref):
    out_ref[...] = we_ref[0:16, 0:128].astype(F32) + wq_ref[0:16, 0:128].astype(F32)


def own_first_kernel(own_ref, we_ref, wq_ref, wkv_ref, x0_ref, q_ref, kv_ref, x_s, n_s):
    means = group_mean_matrix()

    for g in range(GROUPS):
        x_s[:, cols(g)] = dot(own_ref[...], we_ref[:, cols(g)]).astype(BF).astype(F32)

    residual = x_s[...]
    n_s[...] = (residual * row_scale(residual)).astype(BF)
    x0_ref[...] = residual[32:288].astype(BF)

    for g in range(GROUPS):
        query = dot(n_s[32:288, :], wq_ref[:, cols(g)])
        query = query * lax.rsqrt(group_mean(query * query, means) + EPSILON)
        q_ref[:, cols(g)] = (query.astype(BF) * 0.125).astype(BF)
        key = dot(n_s[...], wkv_ref[:, cols(g)])
        key = key * lax.rsqrt(group_mean(key * key, means) + EPSILON)
        kv_ref[:, cols(g)] = key.astype(BF)
        kv_ref[:, cols(g + GROUPS)] = dot(n_s[...], wkv_ref[:, cols(g + GROUPS)]).astype(BF)


def keys_of(kv_ref, rim_ref, block, group):
    rim = rim_ref.shape[0] // 2
    lanes = cols(group)
    return jnp.concatenate(
        [
            kv_ref[64 * block : 64 * block + 128, lanes],
            rim_ref[32 * block : 32 * block + 64, lanes],
            rim_ref[rim + 32 * block : rim + 32 * block + 64, lanes],
        ],
        axis=0,
    )


def first_core_kernel(
    place_ref, mask_ref, a_ref, b_ref, we_ref, wkv_ref, wo_ref, x0_ref, q_ref, kv_ref,
    x1_ref, go_a_ref, go_b_ref,
    p_s, x_s, n_s, rim_s, o_s,
):
    means = group_mean_matrix()
    even = 1 - (place_ref[1] & 1)
    p_s[0:160, :] = dot(widen((160, 112), 2, even), a_ref[...]).astype(BF)
    p_s[160:320, :] = dot(widen((160, 112), 2, 1 - even), b_ref[...]).astype(BF)

    for g in range(GROUPS):
        x_s[:, cols(g)] = dot(p_s[...], we_ref[:, cols(g)]).astype(BF).astype(F32)

    residual = x_s[...]
    n_s[...] = (residual * row_scale(residual)).astype(BF)

    for g in range(GROUPS):
        key = dot(n_s[...], wkv_ref[:, cols(g)])
        key = key * lax.rsqrt(group_mean(key * key, means) + EPSILON)
        rim_s[:, cols(g)] = key.astype(BF)
        rim_s[:, cols(g + GROUPS)] = dot(n_s[...], wkv_ref[:, cols(g + GROUPS)]).astype(BF)

    masks = head_masks()

    for g in range(GROUPS):
        for block in range(4):
            query = stack_heads(q_ref[64 * block : 64 * block + 64, cols(g)], masks)
            key = keys_of(kv_ref, rim_s, block, g)
            value = keys_of(kv_ref, rim_s, block, g + GROUPS)
            weight = jnp.exp(dot(query, key, NT)) * mask_ref[block]
            total = jnp.sum(weight, axis=1, keepdims=True)
            mixed = dot(weight.astype(BF), value) * (1.0 / jnp.where(total > 0, total, 1.0))
            o_s[64 * block : 64 * block + 64, cols(g)] = unstack_heads(mixed).astype(BF)

    n, source = iota((88, 256), 0), iota((88, 256), 1)
    pick_a = jnp.where(edge_token(n, even) + 16 == source, 1.0, 0.0).astype(BF)
    pick_b = jnp.where(edge_token(n, 1 - even) + 16 == source, 1.0, 0.0).astype(BF)

    for g in range(GROUPS):
        total = x0_ref[:, cols(g)].astype(F32) + dot(o_s[...], wo_ref[:, cols(g)])
        total = total.astype(BF)
        x1_ref[:, cols(g)] = total
        go_a_ref[:, cols(g)] = dot(pick_a, total).astype(BF)
        go_b_ref[:, cols(g)] = dot(pick_b, total).astype(BF)


def own_second_kernel(
    place_ref, x1_ref, cot_ref, c_ref, d_ref, wq_ref, wkv_ref, wo_ref,
    q_ref, kv_ref, do_ref, rsq_ref, rsk_ref,
    n_s, c_s,
):
    means = group_mean_matrix()
    residual = x1_ref[...].astype(F32)
    n_s[...] = (residual * row_scale(residual)).astype(BF)
    odd = place_ref[0] & 1
    c_above = jnp.full((32, D), odd, jnp.int32) == 1
    c_edge, d_edge = c_ref[...].astype(F32), d_ref[...].astype(F32)
    c_s[0:32, :] = jnp.where(c_above, c_edge, d_edge).astype(BF)
    c_s[32:160, :] = cot_ref[...]
    c_s[160:192, :] = jnp.where(c_above, d_edge, c_edge).astype(BF)

    for g in range(GROUPS):
        query = dot(n_s[32:224, :], wq_ref[:, cols(g)])
        scale = lax.rsqrt(group_mean(query * query, means) + EPSILON)
        q_ref[:, cols(g)] = ((query * scale).astype(BF) * 0.125).astype(BF)
        rsq_ref[:, cols(g)] = scale[32:160]
        key = dot(n_s[...], wkv_ref[:, cols(g)])
        scale = lax.rsqrt(group_mean(key * key, means) + EPSILON)
        kv_ref[:, cols(g)] = (key * scale).astype(BF)
        rsk_ref[:, cols(g)] = scale[64:192]
        kv_ref[:, cols(g + GROUPS)] = dot(n_s[...], wkv_ref[:, cols(g + GROUPS)]).astype(BF)
        do_ref[:, cols(g)] = dot(c_s[...], wo_ref[cols(g), :], NT).astype(BF)


def head_scale_back(back, normed, scale, means):
    return scale * (back - normed * group_mean(back * normed, means))


def second_core_kernel(
    place_ref, mask_ref, a_ref, b_ref, wkv_ref, q_ref, kv_ref, do_ref,
    o_ref, dq_ref, dkv_ref, go_a_ref, go_b_ref,
    n_s, rim_s, rs_s, db_s, sent_s,
):
    means = group_mean_matrix()
    even = 1 - (place_ref[1] & 1)
    parts = [
        dot(widen((128, 88), 2, right), ref[...])
        for ref, right in ((a_ref, even), (b_ref, 1 - even))
    ]
    residual = jnp.concatenate(parts, axis=0)
    n_s[...] = (residual * row_scale(residual)).astype(BF)

    for g in range(GROUPS):
        key = dot(n_s[...], wkv_ref[:, cols(g)])
        scale = lax.rsqrt(group_mean(key * key, means) + EPSILON)
        rim_s[:, cols(g)] = (key * scale).astype(BF)
        rs_s[0:64, cols(g)] = scale[32:96]
        rs_s[64:128, cols(g)] = scale[160:224]
        rim_s[:, cols(g + GROUPS)] = dot(n_s[...], wkv_ref[:, cols(g + GROUPS)]).astype(BF)

    masks = head_masks()

    for g in range(GROUPS):
        key_backs, value_backs = [], []
        for block in range(3):
            query = stack_heads(q_ref[64 * block : 64 * block + 64, cols(g)], masks)
            key = keys_of(kv_ref, rim_s, block, g)
            value = keys_of(kv_ref, rim_s, block, g + GROUPS)
            out_back = stack_heads(do_ref[64 * block : 64 * block + 64, cols(g)], masks)
            probs = column_softmax(dot(key, query, NT), mask_ref[block])
            probs_low = probs.astype(BF)
            probs_back = dot(value, out_back, NT)
            centre = jnp.sum(probs_back * probs, axis=0, keepdims=True)
            scores_back = (probs * (probs_back - centre)).astype(BF)
            o_ref[64 * block : 64 * block + 64, cols(g)] = unstack_heads(
                dot(probs_low, value, TN)
            ).astype(BF)
            dq_ref[64 * block : 64 * block + 64, cols(g)] = unstack_heads(
                dot(scores_back, key, TN)
            ).astype(BF)
            key_backs.append(dot(scores_back, query))
            value_backs.append(dot(probs_low, out_back))

        def fold(parts):
            def piece(start, half):
                return jnp.concatenate(
                    [
                        parts[0][start + half : start + 2 * half] + parts[1][start : start + half],
                        parts[1][start + half : start + 2 * half] + parts[2][start : start + half],
                    ],
                    axis=0,
                )

            return piece(0, 64), jnp.concatenate([piece(128, 32), piece(192, 32)], axis=0)

        own, rim = fold(key_backs)
        dkv_ref[:, cols(g)] = own.astype(BF)
        normed = jnp.concatenate([rim_s[32:96, cols(g)], rim_s[160:224, cols(g)]], axis=0)
        rim = head_scale_back(rim, normed.astype(F32), rs_s[:, cols(g)], means)
        db_s[:, cols(g)] = rim.astype(BF)
        own, rim = fold(value_backs)
        dkv_ref[:, cols(g + GROUPS)] = own.astype(BF)
        db_s[:, cols(g + GROUPS)] = rim.astype(BF)

    narrow = []
    for right in (even, 1 - even):
        n, m = iota((48, 64), 0), iota((48, 64), 1)
        row = third(n)
        narrow.append(jnp.where(row * 4 + (n - 3 * row) + 1 - right == m, 1.0, 0.0).astype(BF))
    for g in range(2 * GROUPS):
        sent_s[0:48, cols(g)] = dot(narrow[0], db_s[0:64, cols(g)]).astype(BF)
        sent_s[48:96, cols(g)] = dot(narrow[1], db_s[64:128, cols(g)]).astype(BF)
    for g in range(GROUPS):
        back = dot(sent_s[...], wkv_ref[cols(g), :], NT).astype(BF)
        go_a_ref[:, cols(g)] = back[:48]
        go_b_ref[:, cols(g)] = back[48:]


def own_back_kernel(
    x1_ref, o_ref, dq_ref, dkv_ref, q_ref, kv_ref, rsq_ref, rsk_ref, wq_ref, wkv_ref, wo_ref,
    out_ref, dn_ref,
    a_s, b_s,
):
    means = group_mean_matrix()

    for g in range(GROUPS):
        total = x1_ref[64:192, cols(g)].astype(F32) + dot(o_ref[32:160, :], wo_ref[:, cols(g)])
        out_ref[:, cols(g)] = total.astype(BF)
        back = dq_ref[32:160, cols(g)].astype(F32) * 0.125
        normed = q_ref[32:160, cols(g)].astype(F32) * 8.0
        a_s[:, cols(g)] = head_scale_back(back, normed, rsq_ref[:, cols(g)], means).astype(BF)
        back = dkv_ref[:, cols(g)].astype(F32)
        normed = kv_ref[64:192, cols(g)].astype(F32)
        b_s[:, cols(g)] = head_scale_back(back, normed, rsk_ref[:, cols(g)], means).astype(BF)
        b_s[:, cols(g + GROUPS)] = dkv_ref[:, cols(g + GROUPS)]

    for g in range(GROUPS):
        back = dot(a_s[...], wq_ref[cols(g), :], NT) + dot(b_s[...], wkv_ref[cols(g), :], NT)
        dn_ref[:, cols(g)] = back


def last_kernel(place_ref, x1_ref, cot_ref, dn_ref, a_ref, b_ref, out_ref):
    n, source = iota((128, 96), 0), iota((128, 96), 1)
    even = 1 - (place_ref[1] & 1)
    from_a = source < 48
    right = jnp.where(from_a, even, 1 - even)
    token = edge_token(jnp.where(from_a, source, source - 48), right)
    pick = jnp.where(n == token, 1.0, 0.0).astype(BF)
    arrived = jnp.concatenate([a_ref[...], b_ref[...]], axis=0)
    back = dn_ref[...] + dot(pick, arrived)
    residual = x1_ref[64:192, :].astype(F32)
    scale = row_scale(residual)
    normed = residual * scale
    mean = jnp.mean(back * normed, axis=-1, keepdims=True)
    out_ref[...] = (cot_ref[...].astype(F32) + scale * (back - normed * mean)).astype(BF)


def placed(kernel):
    def body(*refs):
        kernel((lax.axis_index("row"), lax.axis_index("col")), *refs)

    return body


def call(kernel, out_shapes, *operands, scratch=(), flops=0, moved=0, small=False, hbm=False):
    vmem = pl.BlockSpec(memory_space=pltpu.VMEM)
    in_specs = [pl.BlockSpec(memory_space=pltpu.HBM) if hbm else vmem] * len(operands)
    if hbm:
        operands = tuple(pltpu.with_memory_space_constraint(x, pltpu.HBM) for x in operands)
    body = placed(kernel) if small else kernel
    shapes = tuple(jax.ShapeDtypeStruct(s, d) for s, d in out_shapes)
    return pl.pallas_call(
        body,
        out_shape=shapes,
        in_specs=in_specs,
        out_specs=tuple(vmem for _ in shapes),
        scratch_shapes=[s if d is None else pltpu.VMEM(s, d) for s, d in scratch],
        compiler_params=pltpu.CompilerParams(vmem_limit_bytes=32 * 1024 * 1024),
        cost_estimate=pl.CostEstimate(flops=flops, bytes_accessed=moved, transcendentals=0),
    )(*operands)


def trade(values, axis, step):
    return lax.ppermute(values, axis, [(i, i ^ step) for i in range(lax.axis_size(axis))])


def trade_sides(go_a, go_b, axis):
    peers = lax.axis_size(axis)
    across = [(i, ((i + 1) ^ 1) - 1) for i in range(peers)]
    b = lax.ppermute(go_b, axis, [(i, j) for i, j in across if 0 <= j < peers])
    return trade(go_a, axis, 1), b


def on_device(patches, tile_slot, w_embed, w_query, w_keyval, w_out, cotangent):
    rows, columns = lax.axis_size("row"), lax.axis_size("col")
    grid_rows, grid_cols = rows * 16, columns * 8
    cot = cotangent.reshape(128, D)
    window = ((96, PIX + 128), BF)

    own, far, edge_c, edge_d = call(
        pack_kernel,
        (window, ((80, PIX + 128), BF), ((32, D), BF), ((32, D), BF)),
        patches, tile_slot.reshape(1, 128), cot,
        small=True, hbm=True,
        scratch=(
            ((1, 128), jnp.int32), ((128, 128), BF), (pltpu.SemaphoreType.DMA((5,)), None)
        ),
    )
    far = trade(far, "row", 4)
    masks = call(
        functools.partial(mask_kernel, grid_rows, grid_cols),
        (((4, 256, 256), F32), ((3, 256, 256), F32)),
        w_keyval,
        small=True,
    )
    sends = call(
        spread_kernel, (window, window, window), own, far, *masks,
        small=True, scratch=(window,),
    )
    (touched,) = call(touch_kernel, (((16, 128), F32),), w_embed, w_query, sends[0])
    arrived = [trade(send, "row", step) for send, step in zip(sends, (2, 3, 1))]
    edge_c, edge_d = trade_sides(edge_c, edge_d, "row")
    own, go_a, go_b = call(
        place_kernel,
        (((320, PIX), BF), ((112, PIX), BF), ((112, PIX), BF)),
        touched, own, far, *arrived,
        small=True,
        scratch=(window,),
    )
    a, b = trade_sides(go_a, go_b, "col")
    x0, queries, keyval = call(
        own_first_kernel,
        (((256, D), BF), ((256, D), BF), ((320, 2 * D), BF)),
        own, w_embed, w_query, w_keyval,
        scratch=(((320, D), F32), ((320, D), BF)),
        flops=8 * 10**9, moved=8 * 10**6,
    )
    x1, go_a, go_b = call(
        first_core_kernel,
        (((256, D), BF), ((88, D), BF), ((88, D), BF)),
        masks[0], a, b, w_embed, w_keyval, w_out, x0, queries, keyval,
        small=True,
        scratch=(
            ((320, PIX), BF), ((320, D), F32), ((320, D), BF), ((320, 2 * D), BF), ((256, D), BF),
        ),
        flops=8 * 10**9, moved=8 * 10**6,
    )
    a, b = trade_sides(go_a, go_b, "col")
    queries, keyval, out_back, query_scale, key_scale = call(
        own_second_kernel,
        (((192, D), BF), ((256, 2 * D), BF), ((192, D), BF), ((128, D), F32), ((128, D), F32)),
        x1, cot, edge_c, edge_d, w_query, w_keyval, w_out,
        small=True,
        scratch=(((256, D), BF), ((192, D), BF)),
        flops=8 * 10**9, moved=8 * 10**6,
    )
    attended, dq, dkv, go_a, go_b = call(
        second_core_kernel,
        (((192, D), BF), ((192, D), BF), ((128, 2 * D), BF), ((48, D), BF), ((48, D), BF)),
        masks[1], a, b, w_keyval, queries, keyval, out_back,
        small=True,
        scratch=(
            ((256, D), BF), ((256, 2 * D), BF), ((128, D), F32), ((128, 2 * D), BF),
            ((96, 2 * D), BF),
        ),
        flops=8 * 10**9, moved=8 * 10**6,
    )
    a, b = trade_sides(go_a, go_b, "col")
    final_tokens, back = call(
        own_back_kernel,
        (((128, D), BF), ((128, D), F32)),
        x1, attended, dq, dkv, queries, keyval, query_scale, key_scale, w_query, w_keyval, w_out,
        scratch=(((128, D), BF), ((128, 2 * D), BF)),
        flops=8 * 10**9, moved=8 * 10**6,
    )
    (input_grad,) = call(last_kernel, (((128, D), BF),), x1, cot, back, a, b, small=True)
    return final_tokens.reshape(16, 8, D), input_grad.reshape(16, 8, D)


def solution(mesh):
    in_specs = (
        P(("row", "col"), None),
        P(("row", "col")),
        P(),
        P(),
        P(),
        P(),
        P("row", "col", None),
    )
    out_specs = (P("row", "col", None), P("row", "col", None))
    return jax.shard_map(
        on_device, mesh=mesh, in_specs=in_specs, out_specs=out_specs, check_vma=False
    )
```

```python
import functools

import jax
import jax.numpy as jnp
from jax import lax
from jax.experimental import pallas as pl
from jax.experimental.pallas import tpu as pltpu
from jax.sharding import PartitionSpec as P

D = 1024
PIX = 768
EPSILON = 1e-06
F32 = jnp.float32
BF = jnp.bfloat16
LANES = 256
GROUPS = D // LANES
NT = (((1,), (1,)), ((), ()))
NN = (((1,), (0,)), ((), ()))
TN = (((0,), (0,)), ((), ()))


def dot(a, b, dims=NN):
    return lax.dot_general(a, b, dims, preferred_element_type=F32)


def iota(shape, axis):
    return lax.broadcasted_iota(jnp.int32, shape, axis)


def group_mean_matrix():
    same = (iota((LANES, LANES), 0) >> 6) == (iota((LANES, LANES), 1) >> 6)
    return jnp.where(same, 1.0 / 64, 0.0).astype(BF)


def group_mean(values, means):
    return dot(values.astype(BF), means)


def row_scale(residual):
    return lax.rsqrt(jnp.mean(residual * residual, axis=-1, keepdims=True) + EPSILON)


def cols(index):
    return slice(index * LANES, index * LANES + LANES)


def head_masks():
    lane = iota((1, LANES), 1) >> 6
    return [jnp.where(lane == h, 1.0, 0.0).astype(BF) for h in range(4)]


def stack_heads(values, masks):
    return jnp.concatenate([values * mask for mask in masks], axis=0)


def unstack_heads(stacked):
    lane = iota((64, LANES), 1) >> 6
    parts = [stacked[64 * h : 64 * h + 64] for h in range(4)]
    low = jnp.where(lane == 0, parts[0], parts[1])
    high = jnp.where(lane == 2, parts[2], parts[3])
    return jnp.where(lane < 2, low, high)


def key_places(key, first_row, col_index, grid_rows, grid_cols):
    right = (key < 192) == ((col_index & 1) == 1)
    rim = key & 63
    key_row = jnp.where(key < 128, key >> 3, rim >> 2)
    rim_col = jnp.where(right, (rim & 3) + 8, (rim & 3) - 4)
    key_col = jnp.where(key < 128, key & 7, rim_col)
    row = first_row + key_row
    col = col_index * 8 + key_col
    inside = (row >= 0) & (row < grid_rows) & (col >= 0) & (col < grid_cols)
    return key_row, key_col, jnp.where(inside, 1.0, 0.0)


def block_masks(axis, first_row, blocks, col_index, grid_rows, grid_cols):
    shapes = (256, 1), (1, 256)
    key, token = iota(shapes[axis], axis), iota(shapes[1 - axis], 1 - axis) & 63
    for block in range(blocks):
        key_row, key_col, inside = key_places(
            key, first_row + 8 * block, col_index, grid_rows, grid_cols
        )
        if block == 0:
            row_gap = key_row - (token >> 3) - 4
            col_gap = key_col - (token & 7)
            near = (row_gap >= -3) & (row_gap <= 3) & (col_gap >= -3) & (col_gap <= 3)
            near = jnp.where(near, 1.0, 0.0)
        yield near * inside


def third(n):
    return (n * 171) >> 9


def edge_token(n, right):
    row = third(n)
    return row * 8 + (n - 3 * row) + 5 * right


def widen(shape, skipped, right):
    m, n = iota(shape, 0), iota(shape, 1)
    slot = (m & 3) - (1 - right)
    match = (((m >> 2) - skipped) * 3 + slot == n) & (slot >= 0) & (slot <= 2)
    return jnp.where(match, 1.0, 0.0).astype(BF)


def column_softmax(scores, mask):
    weight = jnp.exp(scores) * mask
    total = jnp.sum(weight, axis=0, keepdims=True)
    return weight * (1.0 / jnp.where(total > 0, total, 1.0))


def pack_kernel(
    place_ref, patches_ref, slot_ref, cot_ref,
    own_ref, far_ref, go_c_ref, go_d_ref, slot_s, wide_s, sems,
):
    half = place_ref[0] >> 2
    odd = place_ref[0] & 1
    own_rows = pl.ds(pl.multiple_of(16 - 16 * half, 16), 80)
    own_source = pl.ds(pl.multiple_of(48 * half, 16), 80)
    far_source = pl.ds(pl.multiple_of(48 - 48 * half, 16), 80)
    c_rows = pl.ds(pl.multiple_of(96 - 96 * odd, 16), 32)
    d_rows = pl.ds(pl.multiple_of(96 * odd, 16), 32)
    lanes = pl.ds(0, PIX)
    pairs = (
        (slot_ref, slot_s),
        (patches_ref.at[far_source, :], far_ref.at[:, lanes]),
        (patches_ref.at[own_source, :], own_ref.at[own_rows, lanes]),
        (cot_ref.at[c_rows, :], go_c_ref),
        (cot_ref.at[d_rows, :], go_d_ref),
    )
    copies = [pltpu.make_async_copy(*pair, sems.at[i]) for i, pair in enumerate(pairs)]
    for copy in copies:
        copy.start()
    for copy in copies:
        copy.wait()
    wide_s[...] = jnp.broadcast_to(slot_s[...].astype(F32), (128, 128)).T.astype(BF)
    gap = pl.ds(pl.multiple_of(80 * half, 16), 16)
    own_ref[gap, :] = jnp.zeros((16, PIX + 128), BF)
    own_ref[own_rows, PIX:] = wide_s[own_source, :]
    far_ref[:, PIX:] = wide_s[far_source, :]


def far_window(place_ref, far_ref, wide_ref):
    half = place_ref[0] >> 2
    wide_ref[pl.ds(pl.multiple_of(80 * half, 16), 16), :] = jnp.zeros((16, PIX + 128), BF)
    wide_ref[pl.ds(pl.multiple_of(16 - 16 * half, 16), 80), :] = far_ref[...]


def windows(place_ref, own_ref, far_ref, step):
    start = pl.multiple_of(((place_ref[0] & 3) ^ step) * 16, 16)
    return own_ref[pl.ds(start, 48), :], far_ref[pl.ds(start, 48), :]


def spread_kernel(
    place_ref, own_ref, far_ref, mask_a_ref, mask_b_ref, *refs
):
    far_s = refs[3]
    far_window(place_ref, far_ref, far_s)
    for step, out_ref in zip((2, 3, 1), refs):
        near, far = windows(place_ref, own_ref, far_s, step)
        out_ref[0:48, :] = near
        out_ref[48:96, :] = far


def place_kernel(
    place_ref, touched_ref, own_in_ref, far_in_ref, in2_ref, in3_ref, in1_ref,
    own_ref, go_a_ref, go_b_ref, far_s,
):
    far_window(place_ref, far_in_ref, far_s)
    near, far = windows(place_ref, own_in_ref, far_s, 0)
    source = jnp.concatenate([near, far, in2_ref[...], in3_ref[...], in1_ref[...]], axis=0)
    slots = []
    for part in range(3):
        slots.append(source[128 * part : 128 * part + 128, PIX:].astype(F32).T[:8])
    tile = lax.rem(iota((8, 384), 1) >> 4, 3)
    slot = jnp.concatenate(slots, axis=1) + 128.0 * tile.astype(F32)
    source = source[:, :PIX]
    a_right = place_ref[1] & 1

    def pick(position):
        hot = jnp.where(position.astype(F32) == slot[:1], 1.0, 0.0).astype(BF)
        return dot(hot, source).astype(BF)

    own_ref[...] = pick(iota((320, 384), 0) + 32)
    n = iota((112, 384), 0)
    go_a_ref[...] = pick(edge_token(n, a_right) + 48)
    go_b_ref[...] = pick(edge_token(n, 1 - a_right) + 48)


def mask_kernel(grid_rows, grid_cols, place_ref, wkv_ref, first_ref, second_ref):
    row, col = place_ref[0] * 16, place_ref[1]
    for i, mask in enumerate(block_masks(1, row - 12, 4, col, grid_rows, grid_cols)):
        first_ref[i] = mask
    for i, mask in enumerate(block_masks(0, row - 8, 3, col, grid_rows, grid_cols)):
        second_ref[i] = mask


def touch_kernel(we_ref, wq_ref, send_ref, out_ref):
    out_ref[...] = we_ref[0:16, 0:128].astype(F32) + wq_ref[0:16, 0:128].astype(F32)


def own_first_kernel(own_ref, we_ref, wq_ref, wkv_ref, x0_ref, q_ref, kv_ref, x_s, n_s):
    means = group_mean_matrix()

    for g in range(GROUPS):
        x_s[:, cols(g)] = dot(own_ref[...], we_ref[:, cols(g)]).astype(BF).astype(F32)

    residual = x_s[...]
    n_s[...] = (residual * row_scale(residual)).astype(BF)
    x0_ref[...] = residual[32:288].astype(BF)

    for g in range(GROUPS):
        query = dot(n_s[32:288, :], wq_ref[:, cols(g)])
        query = query * lax.rsqrt(group_mean(query * query, means) + EPSILON)
        q_ref[:, cols(g)] = (query.astype(BF) * 0.125).astype(BF)
        key = dot(n_s[...], wkv_ref[:, cols(g)])
        key = key * lax.rsqrt(group_mean(key * key, means) + EPSILON)
        kv_ref[:, cols(g)] = key.astype(BF)
        kv_ref[:, cols(g + GROUPS)] = dot(n_s[...], wkv_ref[:, cols(g + GROUPS)]).astype(BF)


def keys_of(kv_ref, rim_ref, block, group):
    rim = rim_ref.shape[0] // 2
    lanes = cols(group)
    return jnp.concatenate(
        [
            kv_ref[64 * block : 64 * block + 128, lanes],
            rim_ref[32 * block : 32 * block + 64, lanes],
            rim_ref[rim + 32 * block : rim + 32 * block + 64, lanes],
        ],
        axis=0,
    )


def first_core_kernel(
    place_ref, mask_ref, a_ref, b_ref, we_ref, wkv_ref, wo_ref, x0_ref, q_ref, kv_ref,
    x1_ref, go_a_ref, go_b_ref,
    p_s, x_s, n_s, rim_s, o_s,
):
    means = group_mean_matrix()
    a_right = place_ref[1] & 1
    p_s[0:160, :] = dot(widen((160, 112), 2, a_right), a_ref[...]).astype(BF)
    p_s[160:320, :] = dot(widen((160, 112), 2, 1 - a_right), b_ref[...]).astype(BF)

    for g in range(GROUPS):
        x_s[:, cols(g)] = dot(p_s[...], we_ref[:, cols(g)]).astype(BF).astype(F32)

    residual = x_s[...]
    n_s[...] = (residual * row_scale(residual)).astype(BF)

    for g in range(GROUPS):
        key = dot(n_s[...], wkv_ref[:, cols(g)])
        key = key * lax.rsqrt(group_mean(key * key, means) + EPSILON)
        rim_s[:, cols(g)] = key.astype(BF)
        rim_s[:, cols(g + GROUPS)] = dot(n_s[...], wkv_ref[:, cols(g + GROUPS)]).astype(BF)

    masks = head_masks()

    for g in range(GROUPS):
        for block in range(4):
            query = stack_heads(q_ref[64 * block : 64 * block + 64, cols(g)], masks)
            key = keys_of(kv_ref, rim_s, block, g)
            value = keys_of(kv_ref, rim_s, block, g + GROUPS)
            weight = jnp.exp(dot(query, key, NT)) * mask_ref[block]
            total = jnp.sum(weight, axis=1, keepdims=True)
            mixed = dot(weight.astype(BF), value) * (1.0 / jnp.where(total > 0, total, 1.0))
            o_s[64 * block : 64 * block + 64, cols(g)] = unstack_heads(mixed).astype(BF)

    n, source = iota((88, 256), 0), iota((88, 256), 1)
    pick_a = jnp.where(edge_token(n, a_right) + 16 == source, 1.0, 0.0).astype(BF)
    pick_b = jnp.where(edge_token(n, 1 - a_right) + 16 == source, 1.0, 0.0).astype(BF)

    for g in range(GROUPS):
        total = x0_ref[:, cols(g)].astype(F32) + dot(o_s[...], wo_ref[:, cols(g)])
        total = total.astype(BF)
        x1_ref[:, cols(g)] = total
        go_a_ref[:, cols(g)] = dot(pick_a, total).astype(BF)
        go_b_ref[:, cols(g)] = dot(pick_b, total).astype(BF)


def own_second_kernel(
    place_ref, x1_ref, cot_ref, c_ref, d_ref, wq_ref, wkv_ref, wo_ref,
    q_ref, kv_ref, do_ref, rsq_ref, rsk_ref,
    n_s, c_s,
):
    means = group_mean_matrix()
    residual = x1_ref[...].astype(F32)
    n_s[...] = (residual * row_scale(residual)).astype(BF)
    odd = place_ref[0] & 1
    c_above = jnp.full((32, D), odd, jnp.int32) == 1
    c_edge, d_edge = c_ref[...].astype(F32), d_ref[...].astype(F32)
    c_s[0:32, :] = jnp.where(c_above, c_edge, d_edge).astype(BF)
    c_s[32:160, :] = cot_ref[...]
    c_s[160:192, :] = jnp.where(c_above, d_edge, c_edge).astype(BF)

    for g in range(GROUPS):
        query = dot(n_s[32:224, :], wq_ref[:, cols(g)])
        scale = lax.rsqrt(group_mean(query * query, means) + EPSILON)
        q_ref[:, cols(g)] = ((query * scale).astype(BF) * 0.125).astype(BF)
        rsq_ref[:, cols(g)] = scale[32:160]
        key = dot(n_s[...], wkv_ref[:, cols(g)])
        scale = lax.rsqrt(group_mean(key * key, means) + EPSILON)
        kv_ref[:, cols(g)] = (key * scale).astype(BF)
        rsk_ref[:, cols(g)] = scale[64:192]
        kv_ref[:, cols(g + GROUPS)] = dot(n_s[...], wkv_ref[:, cols(g + GROUPS)]).astype(BF)
        do_ref[:, cols(g)] = dot(c_s[...], wo_ref[cols(g), :], NT).astype(BF)


def head_scale_back(back, normed, scale, means):
    return scale * (back - normed * group_mean(back * normed, means))


def second_core_kernel(
    place_ref, mask_ref, a_ref, b_ref, wkv_ref, q_ref, kv_ref, do_ref,
    o_ref, dq_ref, dkv_ref, go_a_ref, go_b_ref,
    n_s, rim_s, rs_s, db_s, sent_s,
):
    means = group_mean_matrix()
    a_right = place_ref[1] & 1
    parts = [
        dot(widen((128, 88), 2, right), ref[...])
        for ref, right in ((a_ref, a_right), (b_ref, 1 - a_right))
    ]
    residual = jnp.concatenate(parts, axis=0)
    n_s[...] = (residual * row_scale(residual)).astype(BF)

    for g in range(GROUPS):
        key = dot(n_s[...], wkv_ref[:, cols(g)])
        scale = lax.rsqrt(group_mean(key * key, means) + EPSILON)
        rim_s[:, cols(g)] = (key * scale).astype(BF)
        rs_s[0:64, cols(g)] = scale[32:96]
        rs_s[64:128, cols(g)] = scale[160:224]
        rim_s[:, cols(g + GROUPS)] = dot(n_s[...], wkv_ref[:, cols(g + GROUPS)]).astype(BF)

    masks = head_masks()

    for g in range(GROUPS):
        key_backs, value_backs = [], []
        for block in range(3):
            query = stack_heads(q_ref[64 * block : 64 * block + 64, cols(g)], masks)
            key = keys_of(kv_ref, rim_s, block, g)
            value = keys_of(kv_ref, rim_s, block, g + GROUPS)
            out_back = stack_heads(do_ref[64 * block : 64 * block + 64, cols(g)], masks)
            probs = column_softmax(dot(key, query, NT), mask_ref[block])
            probs_low = probs.astype(BF)
            probs_back = dot(value, out_back, NT)
            centre = jnp.sum(probs_back * probs, axis=0, keepdims=True)
            scores_back = (probs * (probs_back - centre)).astype(BF)
            o_ref[64 * block : 64 * block + 64, cols(g)] = unstack_heads(
                dot(probs_low, value, TN)
            ).astype(BF)
            dq_ref[64 * block : 64 * block + 64, cols(g)] = unstack_heads(
                dot(scores_back, key, TN)
            ).astype(BF)
            key_backs.append(dot(scores_back, query))
            value_backs.append(dot(probs_low, out_back))

        def fold(parts):
            def piece(start, half):
                return jnp.concatenate(
                    [
                        parts[0][start + half : start + 2 * half] + parts[1][start : start + half],
                        parts[1][start + half : start + 2 * half] + parts[2][start : start + half],
                    ],
                    axis=0,
                )

            return piece(0, 64), jnp.concatenate([piece(128, 32), piece(192, 32)], axis=0)

        own, rim = fold(key_backs)
        dkv_ref[:, cols(g)] = own.astype(BF)
        normed = jnp.concatenate([rim_s[32:96, cols(g)], rim_s[160:224, cols(g)]], axis=0)
        rim = head_scale_back(rim, normed.astype(F32), rs_s[:, cols(g)], means)
        db_s[:, cols(g)] = rim.astype(BF)
        own, rim = fold(value_backs)
        dkv_ref[:, cols(g + GROUPS)] = own.astype(BF)
        db_s[:, cols(g + GROUPS)] = rim.astype(BF)

    narrow = []
    for right in (a_right, 1 - a_right):
        n, m = iota((48, 64), 0), iota((48, 64), 1)
        row = third(n)
        narrow.append(jnp.where(row * 4 + (n - 3 * row) + 1 - right == m, 1.0, 0.0).astype(BF))
    for g in range(2 * GROUPS):
        sent_s[0:48, cols(g)] = dot(narrow[0], db_s[0:64, cols(g)]).astype(BF)
        sent_s[48:96, cols(g)] = dot(narrow[1], db_s[64:128, cols(g)]).astype(BF)
    for g in range(GROUPS):
        back = dot(sent_s[...], wkv_ref[cols(g), :], NT).astype(BF)
        go_a_ref[:, cols(g)] = back[:48]
        go_b_ref[:, cols(g)] = back[48:]


def own_back_kernel(
    x1_ref, o_ref, dq_ref, dkv_ref, q_ref, kv_ref, rsq_ref, rsk_ref, wq_ref, wkv_ref, wo_ref,
    out_ref, dn_ref,
    a_s, b_s,
):
    means = group_mean_matrix()

    for g in range(GROUPS):
        total = x1_ref[64:192, cols(g)].astype(F32) + dot(o_ref[32:160, :], wo_ref[:, cols(g)])
        out_ref[:, cols(g)] = total.astype(BF)
        back = dq_ref[32:160, cols(g)].astype(F32) * 0.125
        normed = q_ref[32:160, cols(g)].astype(F32) * 8.0
        a_s[:, cols(g)] = head_scale_back(back, normed, rsq_ref[:, cols(g)], means).astype(BF)
        back = dkv_ref[:, cols(g)].astype(F32)
        normed = kv_ref[64:192, cols(g)].astype(F32)
        b_s[:, cols(g)] = head_scale_back(back, normed, rsk_ref[:, cols(g)], means).astype(BF)
        b_s[:, cols(g + GROUPS)] = dkv_ref[:, cols(g + GROUPS)]

    for g in range(GROUPS):
        back = dot(a_s[...], wq_ref[cols(g), :], NT) + dot(b_s[...], wkv_ref[cols(g), :], NT)
        dn_ref[:, cols(g)] = back


def last_kernel(place_ref, x1_ref, cot_ref, dn_ref, a_ref, b_ref, out_ref):
    n, source = iota((128, 96), 0), iota((128, 96), 1)
    a_right = place_ref[1] & 1
    from_a = source < 48
    right = jnp.where(from_a, a_right, 1 - a_right)
    token = edge_token(jnp.where(from_a, source, source - 48), right)
    pick = jnp.where(n == token, 1.0, 0.0).astype(BF)
    arrived = jnp.concatenate([a_ref[...], b_ref[...]], axis=0)
    back = dn_ref[...] + dot(pick, arrived)
    residual = x1_ref[64:192, :].astype(F32)
    scale = row_scale(residual)
    normed = residual * scale
    mean = jnp.mean(back * normed, axis=-1, keepdims=True)
    out_ref[...] = (cot_ref[...].astype(F32) + scale * (back - normed * mean)).astype(BF)


def placed(kernel):
    def body(*refs):
        kernel((lax.axis_index("row"), lax.axis_index("col")), *refs)

    return body


def call(kernel, out_shapes, *operands, scratch=(), flops=0, moved=0, small=False, hbm=False):
    vmem = pl.BlockSpec(memory_space=pltpu.VMEM)
    in_specs = [pl.BlockSpec(memory_space=pltpu.HBM) if hbm else vmem] * len(operands)
    if hbm:
        operands = tuple(pltpu.with_memory_space_constraint(x, pltpu.HBM) for x in operands)
    body = placed(kernel) if small else kernel
    shapes = tuple(jax.ShapeDtypeStruct(s, d) for s, d in out_shapes)
    return pl.pallas_call(
        body,
        out_shape=shapes,
        in_specs=in_specs,
        out_specs=tuple(vmem for _ in shapes),
        scratch_shapes=[s if d is None else pltpu.VMEM(s, d) for s, d in scratch],
        compiler_params=pltpu.CompilerParams(vmem_limit_bytes=32 * 1024 * 1024),
        cost_estimate=pl.CostEstimate(flops=flops, bytes_accessed=moved, transcendentals=0),
    )(*operands)


def trade(values, axis, step):
    return lax.ppermute(values, axis, [(i, i ^ step) for i in range(lax.axis_size(axis))])


def trade_across(values, axis):
    peers = lax.axis_size(axis)
    pairs = [(i, ((i + 1) ^ 1) - 1) for i in range(peers)]
    return lax.ppermute(values, axis, [(i, j) for i, j in pairs if 0 <= j < peers])


def trade_sides(go_a, go_b):
    return trade_across(go_a, "col"), trade(go_b, "col", 1)


def on_device(patches, tile_slot, w_embed, w_query, w_keyval, w_out, cotangent):
    rows, columns = lax.axis_size("row"), lax.axis_size("col")
    grid_rows, grid_cols = rows * 16, columns * 8
    cot = cotangent.reshape(128, D)
    window = ((96, PIX + 128), BF)

    own, far, edge_c, edge_d = call(
        pack_kernel,
        (window, ((80, PIX + 128), BF), ((32, D), BF), ((32, D), BF)),
        patches, tile_slot.reshape(1, 128), cot,
        small=True, hbm=True,
        scratch=(
            ((1, 128), jnp.int32), ((128, 128), BF), (pltpu.SemaphoreType.DMA((5,)), None)
        ),
    )
    far = trade(far, "row", 4)
    masks = call(
        functools.partial(mask_kernel, grid_rows, grid_cols),
        (((4, 256, 256), F32), ((3, 256, 256), F32)),
        w_keyval,
        small=True,
    )
    sends = call(
        spread_kernel, (window, window, window), own, far, *masks,
        small=True, scratch=(window,),
    )
    (touched,) = call(touch_kernel, (((16, 128), F32),), w_embed, w_query, sends[0])
    arrived = [trade(send, "row", step) for send, step in zip(sends, (2, 3, 1))]
    edge_c, edge_d = trade(edge_c, "row", 1), trade_across(edge_d, "row")
    own, go_a, go_b = call(
        place_kernel,
        (((320, PIX), BF), ((112, PIX), BF), ((112, PIX), BF)),
        touched, own, far, *arrived,
        small=True,
        scratch=(window,),
    )
    a, b = trade_sides(go_a, go_b)
    x0, queries, keyval = call(
        own_first_kernel,
        (((256, D), BF), ((256, D), BF), ((320, 2 * D), BF)),
        own, w_embed, w_query, w_keyval,
        scratch=(((320, D), F32), ((320, D), BF)),
        flops=8 * 10**9, moved=8 * 10**6,
    )
    x1, go_a, go_b = call(
        first_core_kernel,
        (((256, D), BF), ((88, D), BF), ((88, D), BF)),
        masks[0], a, b, w_embed, w_keyval, w_out, x0, queries, keyval,
        small=True,
        scratch=(
            ((320, PIX), BF), ((320, D), F32), ((320, D), BF), ((320, 2 * D), BF), ((256, D), BF),
        ),
        flops=8 * 10**9, moved=8 * 10**6,
    )
    a, b = trade_sides(go_a, go_b)
    queries, keyval, out_back, query_scale, key_scale = call(
        own_second_kernel,
        (((192, D), BF), ((256, 2 * D), BF), ((192, D), BF), ((128, D), F32), ((128, D), F32)),
        x1, cot, edge_c, edge_d, w_query, w_keyval, w_out,
        small=True,
        scratch=(((256, D), BF), ((192, D), BF)),
        flops=8 * 10**9, moved=8 * 10**6,
    )
    attended, dq, dkv, go_a, go_b = call(
        second_core_kernel,
        (((192, D), BF), ((192, D), BF), ((128, 2 * D), BF), ((48, D), BF), ((48, D), BF)),
        masks[1], a, b, w_keyval, queries, keyval, out_back,
        small=True,
        scratch=(
            ((256, D), BF), ((256, 2 * D), BF), ((128, D), F32), ((128, 2 * D), BF),
            ((96, 2 * D), BF),
        ),
        flops=8 * 10**9, moved=8 * 10**6,
    )
    a, b = trade_sides(go_a, go_b)
    final_tokens, back = call(
        own_back_kernel,
        (((128, D), BF), ((128, D), F32)),
        x1, attended, dq, dkv, queries, keyval, query_scale, key_scale, w_query, w_keyval, w_out,
        scratch=(((128, D), BF), ((128, 2 * D), BF)),
        flops=8 * 10**9, moved=8 * 10**6,
    )
    (input_grad,) = call(last_kernel, (((128, D), BF),), x1, cot, back, a, b, small=True)
    return final_tokens.reshape(16, 8, D), input_grad.reshape(16, 8, D)


def solution(mesh):
    in_specs = (
        P(("row", "col"), None),
        P(("row", "col")),
        P(),
        P(),
        P(),
        P(),
        P("row", "col", None),
    )
    out_specs = (P("row", "col", None), P("row", "col", None))
    return jax.shard_map(
        on_device, mesh=mesh, in_specs=in_specs, out_specs=out_specs, check_vma=False
    )
```
